32 devices in a mesh: dp: 8 (over z, y), bn: 4 (over x, core).
Axes of the slice: x: 2, y: 2, z: 4, core: 2. Of those that a mesh axis runs over, the one named last changes fastest.
Arguments:
- image_small: bfloat16 [64, 10, 10, 1024], P(('dp', 'bn')), may hold values from -6 to 6
- image_mid: bfloat16 [64, 14, 14, 1024], P(('dp', 'bn')), may hold values from -6 to 6
- image_large: bfloat16 [64, 18, 18, 1024], P(('dp', 'bn')), may hold values from -6 to 6
- live_counts: int32 [32, 3], P(('dp', 'bn')), may hold values from 0 to 2, as said below
- reduce_one: bfloat16 [1024, 512], replicated, may hold values from -0.1875 to 0.1875
- spatial_one: bfloat16 [4608, 512], replicated, may hold values from -0.09375 to 0.09375
- expand_one: bfloat16 [512, 2048], replicated, may hold values from -0.25 to 0.25
- squeeze_one: bfloat16 [2048, 128], replicated, may hold values from -0.125 to 0.125
- excite_one: bfloat16 [2048, 128], replicated, may hold values from -0.5 to 0.5
- project_one: bfloat16 [1024, 2048], replicated, may hold values from -0.1875 to 0.1875
- gains_one: float32 [5120], replicated, may hold values from 0.5 to 1.5
- shifts_one: float32 [5120], replicated, may hold values from -3 to 3
- se_bias_one: float32 [2176], replicated, may hold values from -3 to 3
- reduce_two: bfloat16 [2048, 512], replicated, may hold values from -0.125 to 0.125
- spatial_two: bfloat16 [4608, 512], replicated, may hold values from -0.09375 to 0.09375
- expand_two: bfloat16 [512, 2048], replicated, may hold values from -0.25 to 0.25
- squeeze_two: bfloat16 [2048, 128], replicated, may hold values from -0.125 to 0.125
- excite_two: bfloat16 [2048, 128], replicated, may hold values from -0.5 to 0.5
- gains_two: float32 [3072], replicated, may hold values from 0.5 to 1.5
- shifts_two: float32 [3072], replicated, may hold values from -3 to 3
- se_bias_two: float32 [2176], replicated, may hold values from -3 to 3
- cotan_small: bfloat16 [64, 5, 5, 2048], P(('dp', 'bn')), may hold values from -6 to 6
- cotan_mid: bfloat16 [64, 7, 7, 2048], P(('dp', 'bn')), may hold values from -6 to 6
- cotan_large: bfloat16 [64, 9, 9, 2048], P(('dp', 'bn')), may hold values from -6 to 6
Outputs:
- out_small: bfloat16 [64, 5, 5, 2048], P(('dp', 'bn'))
- out_mid: bfloat16 [64, 7, 7, 2048], P(('dp', 'bn'))
- out_large: bfloat16 [64, 9, 9, 2048], P(('dp', 'bn'))
- grad_small: float32 [64, 10, 10, 1024], P(('dp', 'bn'))
- grad_mid: float32 [64, 14, 14, 1024], P(('dp', 'bn'))
- grad_large: float32 [64, 18, 18, 1024], P(('dp', 'bn'))
- grad_matrices_one: float32 [6553600], P(('dp', 'bn'))
- grad_matrices_two: float32 [4980736], P(('dp', 'bn'))
- grad_gains_one: float32 [5120], replicated
- grad_shifts_one: float32 [5120], replicated
- grad_se_bias_one: float32 [2176], replicated
- grad_gains_two: float32 [3072], replicated
- grad_shifts_two: float32 [3072], replicated
- grad_se_bias_two: float32 [2176], replicated
The draws below stay inside these ranges and needn't reach their ends.
Inputs may be any that keep to these rules, and one draw needn't show every extreme that they name: `live_counts`: row d gives, for device d in dp-then-bn order, how many of its slots of the 10, 14 and 18 images (columns 0, 1, 2) hold live images; they are that device's first slots. Column 1 is at least 1. Some device has all 2 slots of every column live.
All inputs are finite; a program needn't handle non-finite values.
Results may differ from the reference program's by a relative error of at most 0.012.
Values sent between devices are 32-bit elements; how exact they have to be, the bound alone decides.
A program may use at most 320 MiB of HBM per device.

```python
import jax
import jax.numpy as jnp
from jax import lax

C_IN = 1024
C_MID = 512
C_OUT = 2048
C_SE = 128
H_SMALL = 10
H_MID = 14
H_LARGE = 18
SLOTS = 2
IMGS = 64
N_DP = 8
DEVICES = 32


def draw_live_counts(key, part):
    key = jax.random.fold_in(key, 7)
    keys = jax.random.split(key, 2)
    counts = jax.random.randint(keys[0], (DEVICES, 3), 0, SLOTS + 1)
    lowest = jnp.array([0, 1, 0], jnp.int32)
    counts = jnp.maximum(counts, lowest[None, :])
    full_row = jax.random.randint(keys[1], (), 0, DEVICES)
    rows = jnp.arange(DEVICES)
    return jnp.where((rows == full_row)[:, None], SLOTS, counts).astype(jnp.int32)


def shard_levels(key, dims, cuts, low, top_value):
    def one(dim, parts):
        draws = jax.random.uniform(jax.random.fold_in(jax.random.fold_in(key, 6), dim), (parts,), jnp.float32, low / len(cuts), top_value / len(cuts))
        return jnp.repeat(jnp.exp(draws), dims[dim] // parts).reshape((-1,) + (1,) * (len(dims) - dim - 1))

    level = one(*cuts[0])
    for cut in cuts[1:]:
        level = level * one(*cut)
    return level


def centred(own_key, extent, scale, reach, pieces=(), kind=jnp.bfloat16):
    drawn = scale * jax.random.normal(own_key, extent, jnp.float32)
    if pieces:
        drawn = drawn * shard_levels(own_key, extent, pieces, -0.22, 0.18)
    return jnp.clip(drawn, -reach, reach).astype(kind)


def setup_inputs(seed: int = 0) -> dict:
    key_list = jax.random.split(jax.random.key(seed), 25)
    return {
        "image_small": centred(key_list[0], (IMGS, H_SMALL, H_SMALL, C_IN), 1.0, 6.0, ((0, 32),)),
        "image_mid": centred(key_list[1], (IMGS, H_MID, H_MID, C_IN), 1.0, 6.0, ((0, 32),)),
        "image_large": centred(key_list[2], (IMGS, H_LARGE, H_LARGE, C_IN), 1.0, 6.0, ((0, 32),)),
        "live_counts": draw_live_counts(jax.random.fold_in(key_list[24], 71), 0),
        "reduce_one": centred(key_list[4], (C_IN, C_MID), C_IN ** -0.5, 0.1875),
        "spatial_one": centred(key_list[5], (9 * C_MID, C_MID), (9 * C_MID) ** -0.5, 0.09375),
        "expand_one": centred(key_list[6], (C_MID, C_OUT), C_MID ** -0.5, 0.25),
        "squeeze_one": centred(key_list[7], (C_OUT, C_SE), C_OUT ** -0.5, 0.125),
        "excite_one": centred(key_list[8], (C_OUT, C_SE), C_SE ** -0.5, 0.5),
        "project_one": centred(key_list[9], (C_IN, C_OUT), C_IN ** -0.5, 0.1875),
        "gains_one": jnp.clip(1.0 + 0.1 * jax.random.normal(key_list[10], (2 * C_MID + 2 * C_OUT,), jnp.float32), 0.5, 1.5),
        "shifts_one": centred(key_list[11], (2 * C_MID + 2 * C_OUT,), 0.3, 3.0, (), jnp.float32),
        "se_bias_one": centred(key_list[12], (C_SE + C_OUT,), 0.3, 3.0, (), jnp.float32),
        "reduce_two": centred(key_list[13], (C_OUT, C_MID), C_OUT ** -0.5, 0.125),
        "spatial_two": centred(key_list[14], (9 * C_MID, C_MID), (9 * C_MID) ** -0.5, 0.09375),
        "expand_two": centred(key_list[15], (C_MID, C_OUT), C_MID ** -0.5, 0.25),
        "squeeze_two": centred(key_list[16], (C_OUT, C_SE), C_OUT ** -0.5, 0.125),
        "excite_two": centred(key_list[17], (C_OUT, C_SE), C_SE ** -0.5, 0.5),
        "gains_two": jnp.clip(1.0 + 0.1 * jax.random.normal(key_list[18], (2 * C_MID + C_OUT,), jnp.float32), 0.5, 1.5),
        "shifts_two": centred(key_list[19], (2 * C_MID + C_OUT,), 0.3, 3.0, (), jnp.float32),
        "se_bias_two": centred(key_list[20], (C_SE + C_OUT,), 0.3, 3.0, (), jnp.float32),
        "cotan_small": centred(key_list[21], (IMGS, H_SMALL // 2, H_SMALL // 2, C_OUT), 1.0, 6.0, ((0, 32),)),
        "cotan_mid": centred(key_list[22], (IMGS, H_MID // 2, H_MID // 2, C_OUT), 1.0, 6.0, ((0, 32),)),
        "cotan_large": centred(key_list[23], (IMGS, H_LARGE // 2, H_LARGE // 2, C_OUT), 1.0, 6.0, ((0, 32),)),
    }


HIGHEST = lax.Precision.HIGHEST
EPSILON = 1e-05

@jax.custom_vjp
def low(v):
    return lax.optimization_barrier(v.astype(jnp.bfloat16)).astype(jnp.float32)

@jax.custom_vjp
def low_back(v):
    return v

def low_keep(v):
    return (low(v), None)

def low_pass(kept, grad):
    return (grad,)

def back_keep(v):
    return (v, None)

def back_low(kept, grad):
    return (low(grad),)
low.defvjp(low_keep, low_pass)
low_back.defvjp(back_keep, back_low)

def pointwise(inputs, weight):
    return jnp.einsum('nhwc,cd->nhwd', inputs, weight, precision=HIGHEST)

def spatial_conv(inputs, weight, stride):
    kernel = weight.reshape(3, 3, inputs.shape[3], weight.shape[1])
    return lax.conv_general_dilated(inputs, kernel, (stride, stride), ((1, 1), (1, 1)), dimension_numbers=('NHWC', 'HWIO', 'NHWC'), precision=HIGHEST)

def sync_norm(values, valid_pixel_masks, norm_gain, norm_shift):
    grouped = []
    spreads = []
    totals = 0.0
    counts = 0.0
    for value, valid_mask in zip(values, valid_pixel_masks):
        group_view = value.reshape((N_DP, -1) + value.shape[1:])
        live_view = valid_mask.reshape(N_DP, -1)
        grouped.append(group_view)
        spreads.append(live_view[:, :, None, None, None])
        totals = totals + lax.optimization_barrier(jnp.sum(group_view * live_view[:, :, None, None, None], axis=(1, 2, 3)))
        counts = counts + lax.optimization_barrier(jnp.sum(live_view, axis=1)) * (value.shape[1] * value.shape[2])
    mean = totals / counts[:, None]
    mean_view = mean[:, None, None, None, :]
    squares = 0.0
    for group_view, live_view in zip(grouped, spreads):
        centered = group_view - mean_view
        squares = squares + lax.optimization_barrier(jnp.sum(centered * centered * live_view, axis=(1, 2, 3)))
    scale = lax.rsqrt(squares / counts[:, None] + EPSILON)
    scale_view = scale[:, None, None, None, :]
    results = []
    for value, group_view in zip(values, grouped):
        normalized_output = (group_view - mean_view) * scale_view * norm_gain + norm_shift
        results.append(normalized_output.reshape(value.shape))
    return results

def excite(values, squeeze, expand, se_bias):
    inner = squeeze.shape[1]
    pooled = lax.optimization_barrier(jnp.mean(values, axis=(1, 2)))
    before = jnp.dot(pooled, squeeze, precision=HIGHEST) + se_bias[:inner]
    after = jnp.dot(jax.nn.silu(before), expand.T, precision=HIGHEST) + se_bias[inner:]
    return values * jax.nn.sigmoid(after)[:, None, None, :]

def block_one(images, valid_pixel_masks, weights):
    reduce_w, spatial_w, expand_w, squeeze_w, excite_w, project_w, norm_gains, shifts, se_bias = weights
    narrow = reduce_w.shape[1]
    broad_width = expand_w.shape[1]
    first = [low_back(pointwise(value, reduce_w)) for value in images]
    first = [low(jax.nn.silu(value)) for value in sync_norm(first, valid_pixel_masks, norm_gains[:narrow], shifts[:narrow])]
    second = [low_back(spatial_conv(value, spatial_w, 2)) for value in first]
    second = [low(jax.nn.silu(value)) for value in sync_norm(second, valid_pixel_masks, norm_gains[narrow:2 * narrow], shifts[narrow:2 * narrow])]
    third = [low_back(pointwise(value, expand_w)) for value in second]
    third = sync_norm(third, valid_pixel_masks, norm_gains[2 * narrow:2 * narrow + broad_width], shifts[2 * narrow:2 * narrow + broad_width])
    branch = [excite(value, squeeze_w, excite_w, se_bias) for value in third]
    shortcut = [low_back(pointwise(value[:, ::2, ::2, :], project_w)) for value in images]
    shortcut = sync_norm(shortcut, valid_pixel_masks, norm_gains[2 * narrow + broad_width:], shifts[2 * narrow + broad_width:])
    return [jax.nn.silu(left + right) for left, right in zip(branch, shortcut)]

def block_two(inputs, valid_pixel_masks, weights):
    reduce_w, spatial_w, expand_w, squeeze_w, excite_w, norm_gains, shifts, se_bias = weights
    narrow = reduce_w.shape[1]
    lowered = [low(value) for value in inputs]
    first = [low_back(pointwise(value, reduce_w)) for value in lowered]
    first = [low(jax.nn.silu(value)) for value in sync_norm(first, valid_pixel_masks, norm_gains[:narrow], shifts[:narrow])]
    second = [low_back(spatial_conv(value, spatial_w, 1)) for value in first]
    second = [low(jax.nn.silu(value)) for value in sync_norm(second, valid_pixel_masks, norm_gains[narrow:2 * narrow], shifts[narrow:2 * narrow])]
    third = [low_back(pointwise(value, expand_w)) for value in second]
    third = sync_norm(third, valid_pixel_masks, norm_gains[2 * narrow:], shifts[2 * narrow:])
    branch = [excite(value, squeeze_w, excite_w, se_bias) for value in third]
    return [jax.nn.silu(left + right) * valid_mask[:, None, None, None] for left, right, valid_mask in zip(branch, inputs, valid_pixel_masks)]

def reference(image_small, image_mid, image_large, live_counts, reduce_one, spatial_one, expand_one, squeeze_one, excite_one, project_one, gains_one, shifts_one, se_bias_one, reduce_two, spatial_two, expand_two, squeeze_two, excite_two, gains_two, shifts_two, se_bias_two, cotan_small, cotan_mid, cotan_large):
    position = jnp.arange(IMGS).astype(jnp.int32)
    device = (position // SLOTS).astype(jnp.int32)
    within = (position % SLOTS).astype(jnp.int32)
    valid_pixel_masks = [(within < live_counts[device, column]).astype(jnp.float32) for column in range(3)]
    floats = [value.astype(jnp.float32) for value in (image_small, image_mid, image_large, reduce_one, spatial_one, expand_one, squeeze_one, excite_one, project_one, gains_one, shifts_one, se_bias_one, reduce_two, spatial_two, expand_two, squeeze_two, excite_two, gains_two, shifts_two, se_bias_two)]

    def forward(*params):
        middle = block_one(list(params[0:3]), valid_pixel_masks, params[3:12])
        return tuple(block_two(middle, valid_pixel_masks, params[12:20]))
    results, pullback = jax.vjp(forward, *floats)
    grads = pullback(tuple((value.astype(jnp.float32) for value in (cotan_small, cotan_mid, cotan_large))))
    matrices_one = jnp.concatenate([grads[k].reshape(-1) for k in range(3, 9)])
    matrices_two = jnp.concatenate([grads[k].reshape(-1) for k in range(12, 17)])
    return (results[0].astype(jnp.bfloat16), results[1].astype(jnp.bfloat16), results[2].astype(jnp.bfloat16), grads[0], grads[1], grads[2], matrices_one, matrices_two, grads[9], grads[10], grads[11], grads[17], grads[18], grads[19])
```

```python
import functools

import jax
import jax.numpy as jnp
import numpy as np
from jax import lax
from jax.experimental import pallas as pl
from jax.experimental.pallas import tpu as pltpu
from jax.sharding import PartitionSpec as P

MESH = pl.DeviceIdType.MESH
HIGHEST = lax.Precision.HIGHEST
EPSILON = 1e-05
TILE = 256
BLOCK = 512
F32 = jnp.float32
BF16 = jnp.bfloat16
VMEM = pl.BlockSpec(memory_space=pltpu.VMEM)
ANY = pl.BlockSpec(memory_space=pl.ANY)
VMEM_BYTES = 62 * 2**20


def dot(a, b):
    return jnp.dot(a, b, preferred_element_type=F32)


def dot_nt(a, b):
    return lax.dot_general(a, b, (((1,), (1,)), ((), ())), preferred_element_type=F32)


def dot_tn(a, b):
    return lax.dot_general(a, b, (((0,), (0,)), ((), ())), preferred_element_type=F32)


def halves(a):
    high = a.astype(BF16)
    return high, (a - high.astype(F32)).astype(BF16)


def silu_slope(value):
    sigma = jax.nn.sigmoid(value)
    return sigma * (1.0 + value * (1.0 - sigma))


def total(v):
    return jnp.sum(v, axis=0, keepdims=True)


def span(j, size=TILE, start=0):
    return pl.ds(pl.multiple_of(start + j * size, 128), size)


class Plan:
    def __init__(self, images, n_bn):
        self.n = n_bn
        self.slots = images[0].shape[0]
        self.sides = [v.shape[1] // 2 for v in images]
        self.segments = []
        start = 0
        for side in self.sides:
            rows = self.slots * side * side
            padded = -(-rows // 16) * 16
            self.segments.append((start, start + padded, side, rows))
            start += padded
        self.rows = start
        shifts = np.zeros((9, start, start), np.float32)
        for begin, _, side, _ in self.segments:
            for tap in range(9):
                for r in range(side):
                    for c in range(side):
                        rr, cc = r + tap // 3 - 1, c + tap % 3 - 1
                        if 0 <= rr < side and 0 <= cc < side:
                            for k in range(self.slots):
                                here = begin + (r * side + c) * self.slots + k
                                there = begin + (rr * side + cc) * self.slots + k
                                shifts[tap, here, there] = 1.0
        self.shifts = shifts.reshape(9 * start, start)

    def mask(self, live_counts):
        pieces = []
        for k, (begin, end, _, rows) in enumerate(self.segments):
            index = jnp.arange(end - begin)
            alive = (index < rows) & (index % self.slots < live_counts[0, k])
            pieces.append(alive.astype(F32))
        return jnp.broadcast_to(jnp.concatenate(pieces)[:, None], (self.rows, TILE))

    def split_parity(self, images):
        pieces = []
        for v, (begin, end, side, rows) in zip(images, self.segments):
            v = v.transpose(1, 2, 0, 3).reshape(side, 2, side, 2, self.slots, -1)
            v = v.transpose(1, 3, 0, 2, 4, 5).reshape(4, rows, -1)
            pieces.append(jnp.pad(v, ((0, 0), (0, end - begin - rows), (0, 0))))
        return jnp.concatenate(pieces, axis=1).reshape(4 * self.rows, -1)

    def join_parity(self, flat):
        flat = flat.reshape(4, self.rows, -1)
        results = []
        for begin, _, side, rows in self.segments:
            v = flat[:, begin : begin + rows].reshape(2, 2, side, side, self.slots, -1)
            v = v.transpose(2, 0, 3, 1, 4, 5).reshape(2 * side, 2 * side, self.slots, -1)
            results.append(v.transpose(2, 0, 1, 3))
        return results

    def flatten(self, maps):
        pieces = []
        for v, (begin, end, side, rows) in zip(maps, self.segments):
            v = v.transpose(1, 2, 0, 3).reshape(rows, -1)
            pieces.append(jnp.pad(v, ((0, end - begin - rows), (0, 0))))
        return jnp.concatenate(pieces, axis=0)

    def unflatten(self, flat):
        results = []
        for begin, _, side, rows in self.segments:
            v = flat[begin : begin + rows].reshape(side, side, self.slots, -1)
            results.append(v.transpose(2, 0, 1, 3))
        return results

    def pooled(self, values):
        results = []
        for begin, end, _, _ in self.segments:
            v = values[begin:end]
            v = jnp.sum(v.reshape((end - begin) // 8, 8, v.shape[1]), axis=0)
            step = self.slots
            while step < 8:
                v = v + pltpu.roll(v, step, 0)
                step *= 2
            results.append(v)
        return results

    def spread(self, k, values, gates):
        rows, width = values.shape
        return (values.reshape(rows // 8, 8, width) * gates[None]).reshape(rows, width)


def enter(n):
    me, dp = lax.axis_index("bn"), lax.axis_index("dp")
    barrier = pltpu.get_barrier_semaphore()
    for k in range(1, n):
        pl.semaphore_signal(
            barrier, inc=1, device_id=(dp, lax.rem(me + k, n)), device_id_type=MESH
        )
    return me


def ready(n):
    pl.semaphore_wait(pltpu.get_barrier_semaphore(), n - 1)


def exchange(n, buffer, send, recv):
    me, dp = lax.axis_index("bn"), lax.axis_index("dp")
    copies = []
    for k in range(1, n):
        copies.append(
            pltpu.make_async_remote_copy(
                src_ref=buffer.at[me],
                dst_ref=buffer.at[me],
                send_sem=send.at[k - 1],
                recv_sem=recv.at[k - 1],
                device_id=(dp, lax.rem(me + k, n)),
                device_id_type=MESH,
            )
        )
    for copy in copies:
        copy.start()
    for copy in copies:
        copy.wait()


def fetch(source, target, sem):
    copy = pltpu.make_async_copy(source, target, sem)
    copy.start()
    return copy


def excite_forward(pooled, squeeze, excite, bias, pre, hidden, gate):
    inner = squeeze.shape[1]
    high, low = halves(pooled[...])
    before = dot(high, squeeze[...]) + dot(low, squeeze[...]) + bias[0:1, 0:inner]
    pre[...] = before
    after = before * jax.nn.sigmoid(before)
    hidden[...] = after
    high, low = halves(after)
    post = dot_nt(high, excite[...]) + dot_nt(low, excite[...]) + bias[0:1, inner:]
    gate[...] = jax.nn.sigmoid(post)


def excite_backward(grad_gate, gate, squeeze, excite, pre, grad_after, grad_before, grad_pooled):
    g = grad_gate[...] * gate[...] * (1.0 - gate[...])
    grad_after[...] = g
    high, low = halves(g)
    hidden = dot(high, excite[...]) + dot(low, excite[...])
    before = hidden * silu_slope(pre[...])
    grad_before[...] = before
    high, low = halves(before)
    grad_pooled[...] = dot_nt(high, squeeze[...]) + dot_nt(low, squeeze[...])


def put(buffer, me, columns, first, second):
    buffer.at[me][0:1, columns] = first
    buffer.at[me][1:2, columns] = second


def statistics(parts, mask, count):
    first = 0.0
    for v in parts:
        first = first + total(v * mask)
    mean = first / count
    second = 0.0
    for v in parts:
        d = (v - mean) * mask
        second = second + total(d * d)
    return first, second


def combine(buffer, columns, counts, level):
    n = len(counts)
    first, count = 0.0, 0.0
    for r in range(n):
        first = first + buffer[r, 0:1, columns]
        count = count + counts[r] * level
    mean = first / count
    squares = 0.0
    for r in range(n):
        own = counts[r] * level
        d = buffer[r, 0:1, columns] / own - mean
        squares = squares + buffer[r, 1:2, columns] + own * (d * d)
    return mean, lax.rsqrt(squares / count + EPSILON)


def gathered(n, buffer, columns):
    value = buffer[0, 0:2, columns]
    for r in range(1, n):
        value = value + buffer[r, 0:2, columns]
    return value[0:1], value[1:2]


def norm_back(g, xhat, mask, factor, first, second, inverse):
    return factor * (g - mask * ((first + xhat * second) * inverse))


NARROW, BROAD = 512, 2048
A, B, C, S, D, E, F = 0, 512, 1024, 3072, 5120, 5632, 6144


def forward_kernel(plan, *refs):
    (x, cot, mask, shifts, g1, b1, sb1, g2, b2, sb2) = refs[:10]
    (hr1, hp1, hs1, he1, hq1, hx1, hr2, hs2, he2, hq2, hx2) = refs[10:21]
    (out, xa, ha, xb, hb, xc, xs, hm, xd, hd, gs, he, dzf, moved) = refs[21:35]
    (scales, inverse, sums) = refs[35:38]
    (pool1, pre1, hid1, gate1, pool2, hid2, after2, before2) = refs[38:46]
    (wr1, wp1, ws, we1, wq1, wx1, wr2, we2, wq2, wx2) = refs[46:56]
    (mid, xe, xf, ge, dze, gate2, pre2, gg, gp) = refs[56:65]
    bufs = refs[65:73]
    wsem, send, recv = refs[73:]
    n, rows = plan.n, plan.rows
    me = enter(n)
    pairs = [(hr1, wr1), (hp1, wp1), (hs1, ws), (he1, we1), (hq1, wq1), (hx1, wx1)]
    pairs += [(hr2, wr2), (he2, we2), (hq2, wq2), (hx2, wx2)]
    loads = [fetch(s, t, wsem.at[k]) for k, (s, t) in enumerate(pairs)]
    m = mask[...]
    own = total(m)
    parity = [slice(p * rows, (p + 1) * rows) for p in range(4)]
    extra = pl.ds(NARROW + BROAD, TILE)
    put(bufs[0], me, extra, own, own)

    loads[0].wait()

    @pl.loop(0, NARROW // TILE)
    def _(j):
        w = wr1[:, span(j)]
        for p in parity:
            xa[p, span(j)] = dot(x[p, :], w)
        first, second = statistics([xa[p, span(j)] for p in parity], m, own * 4.0)
        put(bufs[0], me, span(j), first, second)

    loads[1].wait()

    @pl.loop(0, BROAD // TILE)
    def _(j):
        z = dot(x[parity[0], :], wp1[:, span(j)])
        xs[:, span(j)] = z
        first, second = statistics([z], m, own)
        put(bufs[0], me, span(j, start=NARROW), first, second)

    ready(n)
    exchange(n, bufs[0], send.at[0], recv.at[0])
    counts = [bufs[0][r, 0:1, extra] for r in range(n)]
    everyone = counts[0]
    for r in range(1, n):
        everyone = everyone + counts[r]
    inverse[...] = 1.0 / everyone

    @pl.loop(0, NARROW // TILE)
    def _(j):
        mean, scale = combine(bufs[0], span(j), counts, 4.0)
        scales[0:1, span(j, start=A)] = scale
        for p in parity:
            v = (xa[p, span(j)] - mean) * scale
            xa[p, span(j)] = v
            v = v * g1[0:1, span(j)] + b1[0:1, span(j)]
            ha[p, span(j)] = (v * jax.nn.sigmoid(v)).astype(BF16)

    @pl.loop(0, BROAD // TILE)
    def _(j):
        mean, scale = combine(bufs[0], span(j, start=NARROW), counts, 1.0)
        scales[0:1, span(j, start=S)] = scale
        xs[:, span(j)] = (xs[:, span(j)] - mean) * scale

    def narrow_norm(target, low, buffer, k, gain, shift, offset, where):
        @pl.loop(0, NARROW // TILE)
        def _(j):
            first, second = statistics([target[:, span(j)]], m, own)
            put(buffer, me, span(j), first, second)

        exchange(n, buffer, send.at[k], recv.at[k])

        @pl.loop(0, NARROW // TILE)
        def _(j):
            mean, scale = combine(buffer, span(j), counts, 1.0)
            scales[0:1, span(j, start=where)] = scale
            v = (target[:, span(j)] - mean) * scale
            target[:, span(j)] = v
            v = v * gain[0:1, span(j, start=offset)] + shift[0:1, span(j, start=offset)]
            low[:, span(j)] = (v * jax.nn.sigmoid(v)).astype(BF16)

    def broad_norm(source, weight, target, buffer, k, gain, shift, offset, where, pool):
        @pl.loop(0, BROAD // TILE)
        def _(j):
            z = dot(source[...], weight[:, span(j)])
            target[:, span(j)] = z
            first, second = statistics([z], m, own)
            put(buffer, me, span(j), first, second)

        exchange(n, buffer, send.at[k], recv.at[k])

        @pl.loop(0, BROAD // TILE)
        def _(j):
            mean, scale = combine(buffer, span(j), counts, 1.0)
            scales[0:1, span(j, start=where)] = scale
            v = (target[:, span(j)] - mean) * scale
            target[:, span(j)] = v
            v = v * gain[0:1, span(j, start=offset)] + shift[0:1, span(j, start=offset)]
            for k3, pooled in enumerate(plan.pooled(v * m)):
                side = plan.sides[k3]
                pool[8 * k3 : 8 * k3 + 8, span(j)] = pooled / (side * side)

    loads[2].wait()
    xb[...] = jnp.zeros_like(xb)

    @pl.loop(0, 9)
    def _(t):
        i, j = t // 3, t % 3
        phase = 2 * ((i + 1) % 2) + (j + 1) % 2
        shift = 3 * ((i + 1) // 2) + (j + 1) // 2
        moved_in = dot(
            shifts[pl.ds(pl.multiple_of(shift * rows, 16), rows), :],
            ha[pl.ds(pl.multiple_of(phase * rows, 16), rows), :],
        ).astype(BF16)
        xb[...] += dot(moved_in, ws[pl.ds(pl.multiple_of(t * NARROW, 128), NARROW), :])

    second_load = fetch(hs2, ws, wsem.at[10])
    narrow_norm(xb, hb, bufs[1], 1, g1, b1, NARROW, B)

    loads[3].wait()
    broad_norm(hb, we1, xc, bufs[2], 2, g1, b1, 2 * NARROW, C, pool1)
    loads[4].wait()
    loads[5].wait()
    excite_forward(pool1, wq1, wx1, sb1, pre1, hid1, gate1)

    @pl.loop(0, BROAD // TILE)
    def _(j):
        at, at_s = span(j, start=2 * NARROW), span(j, start=2 * NARROW + BROAD)
        for k, (a, b, _, _) in enumerate(plan.segments):
            v = xc[a:b, span(j)] * g1[0:1, at] + b1[0:1, at]
            v = plan.spread(k, v, gate1[8 * k : 8 * k + 8, span(j)])
            v = v + xs[a:b, span(j)] * g1[0:1, at_s] + b1[0:1, at_s]
            v = v * jax.nn.sigmoid(v)
            mid[a:b, span(j)] = v
            hm[a:b, span(j)] = v.astype(BF16)

    loads[6].wait()

    @pl.loop(0, NARROW // TILE)
    def _(j):
        xd[:, span(j)] = dot(hm[...], wr2[:, span(j)])

    narrow_norm(xd, hd, bufs[3], 3, g2, b2, 0, D)

    second_load.wait()
    xe[...] = jnp.zeros_like(xe)

    @pl.loop(0, 9)
    def _(t):
        moved_in = dot(
            shifts[pl.ds(pl.multiple_of(t * rows, 16), rows), :], hd[...]
        ).astype(BF16)
        xe[...] += dot(moved_in, ws[pl.ds(pl.multiple_of(t * NARROW, 128), NARROW), :])

    narrow_norm(xe, he, bufs[4], 4, g2, b2, NARROW, E)
    loads[7].wait()
    broad_norm(he, we2, xf, bufs[5], 5, g2, b2, 2 * NARROW, F, pool2)
    loads[8].wait()
    loads[9].wait()
    excite_forward(pool2, wq2, wx2, sb2, pre2, hid2, gate2)

    @pl.loop(0, BROAD // TILE)
    def _(j):
        at = span(j, start=2 * NARROW)
        for k, (a, b, _, _) in enumerate(plan.segments):
            v = xf[a:b, span(j)] * g2[0:1, at] + b2[0:1, at]
            u = plan.spread(k, v, gate2[8 * k : 8 * k + 8, span(j)]) + mid[a:b, span(j)]
            sigma = jax.nn.sigmoid(u)
            mk = mask[a:b, :]
            out[a:b, span(j)] = (u * sigma * mk).astype(BF16)
            g = cot[a:b, span(j)].astype(F32) * mk * (sigma * (1.0 + u * (1.0 - sigma)))
            gs[a:b, span(j)] = g
            mid[a:b, span(j)] = g * v
        for k, pooled in enumerate(plan.pooled(mid[:, span(j)])):
            gg[8 * k : 8 * k + 8, span(j)] = pooled

    excite_backward(gg, gate2, wq2, wx2, pre2, after2, before2, gp)

    @pl.loop(0, BROAD // TILE)
    def _(j):
        for k, (a, b, side, _) in enumerate(plan.segments):
            at = slice(8 * k, 8 * k + 8)
            g = plan.spread(k, gs[a:b, span(j)], gate2[at, span(j)])
            mid[a:b, span(j)] = g + plan.spread(
                k, mask[a:b, :], gp[at, span(j)] * (1.0 / (side * side))
            )
        g = mid[:, span(j)]
        first, second = total(g), total(g * xf[:, span(j)])
        put(bufs[6], me, span(j), first, second)
        sums[0:1, span(j)] = first
        sums[1:2, span(j)] = second

    exchange(n, bufs[6], send.at[6], recv.at[6])

    @pl.loop(0, BROAD // TILE)
    def _(j):
        first, second = gathered(n, bufs[6], span(j))
        factor = g2[0:1, span(j, start=2 * NARROW)] * scales[0:1, span(j, start=F)]
        dzf[:, span(j)] = norm_back(
            mid[:, span(j)], xf[:, span(j)], mask[...], factor, first, second, inverse[...]
        ).astype(BF16)

    @pl.loop(0, NARROW // TILE)
    def _(j):
        at = span(j, start=NARROW)
        v = xe[:, span(j)]
        g = dot_nt(dzf[...], we2[span(j), :]) * silu_slope(v * g2[0:1, at] + b2[0:1, at])
        ge[:, span(j)] = g
        first, second = total(g), total(g * v)
        put(bufs[7], me, span(j), first, second)
        sums[0:1, span(j, start=BROAD)] = first
        sums[1:2, span(j, start=BROAD)] = second

    exchange(n, bufs[7], send.at[7], recv.at[7])

    @pl.loop(0, NARROW // TILE)
    def _(j):
        first, second = gathered(n, bufs[7], span(j))
        factor = g2[0:1, span(j, start=NARROW)] * scales[0:1, span(j, start=E)]
        dze[:, span(j)] = norm_back(
            ge[:, span(j)], xe[:, span(j)], mask[...], factor, first, second, inverse[...]
        ).astype(BF16)

    @pl.loop(0, 9)
    def _(t):
        at = pl.ds(pl.multiple_of(t * rows, 16), rows)
        moved[at, :] = dot(shifts[at, :], dze[...]).astype(BF16)


def middle_kernel(plan, *refs):
    (mask, moved, xd, gs, xc, xs, gate1, pre1, scales, inverse, g1, b1, g2, b2) = refs[:14]
    (hs2, hr2, hq1, hx1) = refs[14:18]
    (dzd, dzc, dzs, after1, before1, sums) = refs[18:24]
    (ws, wr2, wq1, wx1, gd, gm, gg, gp, buf0, buf1, wsem, send, recv) = refs[24:]
    n, rows = plan.n, plan.rows
    me = enter(n)
    pairs = [(hs2, ws), (hr2, wr2), (hq1, wq1), (hx1, wx1)]
    loads = [fetch(s, t, wsem.at[k]) for k, (s, t) in enumerate(pairs)]

    loads[0].wait()
    gd[...] = jnp.zeros_like(gd)

    @pl.loop(0, 9)
    def _(t):
        gd[...] += dot_nt(
            moved[pl.ds(pl.multiple_of((8 - t) * rows, 16), rows), :],
            ws[pl.ds(pl.multiple_of(t * NARROW, 128), NARROW), :],
        )

    @pl.loop(0, NARROW // TILE)
    def _(j):
        v = xd[:, span(j)]
        g = gd[:, span(j)] * silu_slope(v * g2[0:1, span(j)] + b2[0:1, span(j)])
        gd[:, span(j)] = g
        first, second = total(g), total(g * v)
        put(buf0, me, span(j), first, second)
        sums[0:1, span(j)] = first
        sums[1:2, span(j)] = second

    ready(n)
    exchange(n, buf0, send.at[0], recv.at[0])

    @pl.loop(0, NARROW // TILE)
    def _(j):
        first, second = gathered(n, buf0, span(j))
        factor = g2[0:1, span(j)] * scales[0:1, span(j, start=D)]
        dzd[:, span(j)] = norm_back(
            gd[:, span(j)], xd[:, span(j)], mask[...], factor, first, second, inverse[...]
        ).astype(BF16)

    loads[1].wait()

    @pl.loop(0, BROAD // TILE)
    def _(j):
        at, at_s = span(j, start=2 * NARROW), span(j, start=2 * NARROW + BROAD)
        gm[:, span(j)] = gs[:, span(j)] + dot_nt(dzd[...], wr2[span(j), :])
        products = []
        for k, (a, b, _, _) in enumerate(plan.segments):
            v = xc[a:b, span(j)] * g1[0:1, at] + b1[0:1, at]
            u = plan.spread(k, v, gate1[8 * k : 8 * k + 8, span(j)])
            u = u + xs[a:b, span(j)] * g1[0:1, at_s] + b1[0:1, at_s]
            g = gm[a:b, span(j)] * silu_slope(u)
            gm[a:b, span(j)] = g
            products.append(g * v)
        for k, pooled in enumerate(plan.pooled(jnp.concatenate(products, axis=0))):
            gg[8 * k : 8 * k + 8, span(j)] = pooled
        g = gm[:, span(j)]
        first, second = total(g), total(g * xs[:, span(j)])
        put(buf1, me, span(j, start=BROAD), first, second)
        sums[0:1, span(j, start=NARROW + BROAD)] = first
        sums[1:2, span(j, start=NARROW + BROAD)] = second

    loads[2].wait()
    loads[3].wait()
    excite_backward(gg, gate1, wq1, wx1, pre1, after1, before1, gp)

    def through_gate(j):
        pieces = []
        for k, (a, b, side, _) in enumerate(plan.segments):
            at = slice(8 * k, 8 * k + 8)
            pieces.append(
                plan.spread(k, gm[a:b, span(j)], gate1[at, span(j)])
                + plan.spread(k, mask[a:b, :], gp[at, span(j)] * (1.0 / (side * side)))
            )
        return jnp.concatenate(pieces, axis=0)

    @pl.loop(0, BROAD // TILE)
    def _(j):
        g = through_gate(j)
        first, second = total(g), total(g * xc[:, span(j)])
        put(buf1, me, span(j), first, second)
        sums[0:1, span(j, start=NARROW)] = first
        sums[1:2, span(j, start=NARROW)] = second

    exchange(n, buf1, send.at[1], recv.at[1])

    @pl.loop(0, BROAD // TILE)
    def _(j):
        m, inv = mask[...], inverse[...]
        first, second = gathered(n, buf1, span(j))
        factor = g1[0:1, span(j, start=2 * NARROW)] * scales[0:1, span(j, start=C)]
        dzc[:, span(j)] = norm_back(
            through_gate(j), xc[:, span(j)], m, factor, first, second, inv
        ).astype(BF16)
        first, second = gathered(n, buf1, span(j, start=BROAD))
        factor = g1[0:1, span(j, start=2 * NARROW + BROAD)] * scales[0:1, span(j, start=S)]
        dzs[:, span(j)] = norm_back(
            gm[:, span(j)], xs[:, span(j)], m, factor, first, second, inv
        ).astype(BF16)


def last_kernel(plan, *refs):
    (mask, shifts, dzc, xb, xa, scales, inverse, g1, b1) = refs[:9]
    (he1, hs1) = refs[9:11]
    (moved, dza, sums) = refs[11:14]
    (we1, ws, gb, dzb, ga, buf0, buf1, wsem, send, recv) = refs[14:]
    n, rows = plan.n, plan.rows
    me = enter(n)
    loads = [fetch(s, t, wsem.at[k]) for k, (s, t) in enumerate([(he1, we1), (hs1, ws)])]
    loads[0].wait()

    @pl.loop(0, NARROW // TILE)
    def _(j):
        at = span(j, start=NARROW)
        v = xb[:, span(j)]
        g = dot_nt(dzc[...], we1[span(j), :]) * silu_slope(v * g1[0:1, at] + b1[0:1, at])
        gb[:, span(j)] = g
        first, second = total(g), total(g * v)
        put(buf0, me, span(j), first, second)
        sums[0:1, at] = first
        sums[1:2, at] = second

    ready(n)
    exchange(n, buf0, send.at[0], recv.at[0])

    @pl.loop(0, NARROW // TILE)
    def _(j):
        first, second = gathered(n, buf0, span(j))
        at = span(j, start=NARROW)
        factor = g1[0:1, at] * scales[0:1, span(j, start=B)]
        dzb[:, span(j)] = norm_back(
            gb[:, span(j)], xb[:, span(j)], mask[...], factor, first, second, inverse[...]
        ).astype(BF16)

    moved[0:rows, :] = dzb[...]
    for slot, tap in ((1, 5), (2, 7), (3, 8)):
        moved[slot * rows : (slot + 1) * rows, :] = dot(
            shifts[tap * rows : (tap + 1) * rows, :], dzb[...]
        ).astype(BF16)

    loads[1].wait()
    ga[...] = jnp.zeros_like(ga)

    @pl.loop(0, 9)
    def _(t):
        i, j = t // 3, t % 3
        phase = 2 * ((i + 1) % 2) + (j + 1) % 2
        slot = 2 * (1 - (i + 1) // 2) + 1 - (j + 1) // 2
        at = pl.ds(pl.multiple_of(phase * rows, 16), rows)
        ga[at, :] += dot_nt(
            moved[pl.ds(pl.multiple_of(slot * rows, 16), rows), :],
            ws[pl.ds(pl.multiple_of(t * NARROW, 128), NARROW), :],
        )

    parity = [slice(p * rows, (p + 1) * rows) for p in range(4)]

    @pl.loop(0, NARROW // TILE)
    def _(j):
        first, second = 0.0, 0.0
        for p in parity:
            v = xa[p, span(j)]
            g = ga[p, span(j)] * silu_slope(v * g1[0:1, span(j)] + b1[0:1, span(j)])
            ga[p, span(j)] = g
            first = first + total(g)
            second = second + total(g * v)
        put(buf1, me, span(j), first, second)
        sums[0:1, span(j)] = first
        sums[1:2, span(j)] = second

    exchange(n, buf1, send.at[1], recv.at[1])

    @pl.loop(0, NARROW // TILE)
    def _(j):
        first, second = gathered(n, buf1, span(j))
        factor = g1[0:1, span(j)] * scales[0:1, span(j, start=A)]
        inv = inverse[...] * 0.25
        for p in parity:
            dza[p, span(j)] = norm_back(
                ga[p, span(j)], xa[p, span(j)], mask[...], factor, first, second, inv
            ).astype(BF16)


STAGES = 6


def weight_kernel(names, jobs, pieces_of, n_out, *refs):
    named = dict(zip(names, refs[: len(names)]))
    outs = refs[len(names) : len(names) + n_out]
    stage, spare, sem = refs[len(names) + n_out :]
    core = lax.rem(lax.axis_index("bn"), 2)
    waiting = [[] for _ in range(STAGES)]
    for index, (start, make) in enumerate(jobs):
        slot = index % STAGES
        for copy in waiting[slot]:
            copy.wait()
        waiting[slot] = []
        make(named, stage.at[slot], spare)
        for k, (low, high, parity, at) in enumerate(pieces_of(start)):
            source = stage.at[slot, low:high]
            copies = [
                pltpu.make_async_copy(source, out.at[at[0], at[1] : at[1] + high - low], sem.at[slot, k])
                for out in outs
            ]
            if n_out == 1:
                copies[0].start()
            else:
                pl.when(core == parity)(copies[0].start)
                pl.when(core != parity)(copies[1].start)
            waiting[slot].append(copies[0])
    for copies in waiting:
        for copy in copies:
            copy.wait()


def make_plain(left, right, column, left_rows=None, right_rows=None):
    def make(named, stage, spare):
        a, b = named[left], named[right]
        a_rows = slice(0, a.shape[0]) if left_rows is None else slice(*left_rows)
        b_rows = slice(0, b.shape[0]) if right_rows is None else slice(*right_rows)
        stage[...] = dot_tn(a[a_rows, column : column + BLOCK], b[b_rows, :])

    return make


def make_wide(left, right, column, left_rows=None):
    def make(named, stage, spare):
        a, b = named[left], named[right]
        a_rows = slice(0, a.shape[0]) if left_rows is None else slice(*left_rows)
        count = BROAD // BLOCK
        lhs = a[a_rows, column : column + BLOCK // count]
        for q in range(count):
            value = dot_tn(lhs, b[:, q * BLOCK : (q + 1) * BLOCK])
            for c in range(BLOCK // 128):
                at = pl.ds(c * BLOCK + q, BLOCK // count, stride=count)
                spare[at, :] = value[:, c * 128 : (c + 1) * 128]
        for c in range(BLOCK // 128):
            stage[:, c * 128 : (c + 1) * 128] = spare[c * BLOCK : (c + 1) * BLOCK, :]

    return make


def make_thin(left, right, repeat):
    def make(named, stage, spare):
        value = lax.dot_general(
            named[left][...],
            named[right][...],
            (((0,), (0,)), ((), ())),
            precision=HIGHEST,
            preferred_element_type=F32,
        )
        width = value.shape[1]
        count = BLOCK // width
        spare[...] = value * (1.0 / repeat)
        for q in range(count):
            stage[:, q * width : (q + 1) * width] = spare[pl.ds(q, BLOCK, stride=count), :]

    return make


def weight_grads(named, jobs, low, high, rows, split):
    todo = [j for j in jobs if j[0] < high and j[0] + BLOCK > low]

    def pieces_of(start):
        pieces = []
        if not split:
            return [(0, BLOCK, 0, (0, start))]
        for k in range(max(start, low) // rows, -(-min(start + BLOCK, high) // rows)):
            a, b = max(start, low, k * rows), min(start + BLOCK, high, (k + 1) * rows)
            where = (k - low // rows) // 2
            pieces.append((a - start, b - start, k % 2, (where, a - k * rows)))
        return pieces

    names = list(named)
    if split:
        shape = jax.ShapeDtypeStruct(((high - low) // rows // 2, rows, BLOCK), F32)
    else:
        shape = jax.ShapeDtypeStruct((1, high - low, BLOCK), F32)
    n_out = 2 if split else 1
    most = max(len(pieces_of(j[0])) for j in todo)
    flops = 2 * len(todo) * BLOCK * BLOCK * 352
    return pl.pallas_call(
        functools.partial(weight_kernel, names, todo, pieces_of, n_out),
        out_shape=[shape] * n_out,
        in_specs=[VMEM] * len(names),
        out_specs=[ANY] * n_out,
        scratch_shapes=[
            pltpu.VMEM((STAGES, BLOCK, BLOCK), F32),
            pltpu.VMEM((BROAD, 128), F32),
            pltpu.SemaphoreType.DMA((STAGES, most)),
        ],
        compiler_params=pltpu.CompilerParams(vmem_limit_bytes=VMEM_BYTES),
        cost_estimate=pl.CostEstimate(
            flops=flops, bytes_accessed=len(todo) * BLOCK * BLOCK * 4, transcendentals=0
        ),
    )(*named.values())


def call(kernel, plan, args, n_any, outs, scratch, collective_id, cost):
    n_vmem = len(args) - n_any
    return pl.pallas_call(
        functools.partial(kernel, plan),
        out_shape=outs,
        in_specs=[VMEM] * n_vmem + [ANY] * n_any,
        out_specs=[VMEM] * len(outs),
        scratch_shapes=scratch,
        compiler_params=pltpu.CompilerParams(
            collective_id=collective_id, has_side_effects=True, vmem_limit_bytes=VMEM_BYTES
        ),
        cost_estimate=pl.CostEstimate(flops=cost, bytes_accessed=cost // 500, transcendentals=0),
    )(*args)


def bits_of(size):
    return size.bit_length() - 1


def scatter_half(keep, send, top, n_dp, n_bn):
    dp, bn = lax.axis_index("dp"), lax.axis_index("bn")
    axes = ("dp", "bn")

    def flip(axis, bit):
        pairs = []
        for d in range(n_dp):
            for b in range(n_bn):
                e, c = (d ^ (1 << bit), b) if axis == "dp" else (d, b ^ (1 << bit))
                pairs.append((d * n_bn + b, e * n_bn + c))
        return pairs

    rows = keep.shape[1]
    value = keep + lax.ppermute(send, axes, flip("bn", 0))
    labels = [("dp", k) for k in reversed(range(bits_of(n_dp) - 1))]
    labels += [("bn", k) for k in reversed(range(1, bits_of(n_bn)))]
    along = [label for label in labels if label[0] == "bn"]
    across = [label for label in labels if label == ("dp", 0)]
    rest = [label for label in reversed(labels) if label[0] == "dp" and label[1] > 0]
    results = []
    for part, order in enumerate((along + across + rest, across + along + rest)):
        v = value[:, part * rows // 2 : (part + 1) * rows // 2]
        v = v.reshape((2,) * len(labels) + (rows // 2, BLOCK))
        left = list(labels)
        for label in order:
            axis = left.index(label)
            mine = lax.rem((dp if label[0] == "dp" else bn) // (1 << label[1]), 2)
            away = lax.dynamic_index_in_dim(v, 1 - mine, axis, keepdims=False)
            own = lax.dynamic_index_in_dim(v, mine, axis, keepdims=False)
            v = own + lax.ppermute(away, axes, flip(*label))
            left.pop(axis)
        bit = bits_of(n_dp) - 1
        pairs = [(s, t) for s, t in flip("dp", bit) if (t // n_bn) >> bit == top]
        results.append(v + lax.ppermute(v, axes, pairs))
    return jnp.concatenate(results, axis=0)


def local(
    n_dp,
    n_bn,
    image_small,
    image_mid,
    image_large,
    live_counts,
    reduce_one,
    spatial_one,
    expand_one,
    squeeze_one,
    excite_one,
    project_one,
    gains_one,
    shifts_one,
    se_bias_one,
    reduce_two,
    spatial_two,
    expand_two,
    squeeze_two,
    excite_two,
    gains_two,
    shifts_two,
    se_bias_two,
    cotan_small,
    cotan_mid,
    cotan_large,
):
    plan = Plan([image_small, image_mid, image_large], n_bn)
    rows = plan.rows
    x = plan.split_parity([image_small, image_mid, image_large])
    cot = plan.flatten([cotan_small, cotan_mid, cotan_large])
    mask = plan.mask(live_counts)
    shifts = jnp.asarray(plan.shifts, BF16)
    g1, b1, sb1 = gains_one[None], shifts_one[None], se_bias_one[None]
    g2, b2, sb2 = gains_two[None], shifts_two[None], se_bias_two[None]

    def f32(*shape):
        return jax.ShapeDtypeStruct(shape, F32)

    def b16(*shape):
        return jax.ShapeDtypeStruct(shape, BF16)

    def group(width):
        return pltpu.VMEM((n_bn, 2, width), F32)

    inner = squeeze_one.shape[1]
    images = 8 * len(plan.segments)
    sems = pltpu.SemaphoreType.DMA
    first = call(
        forward_kernel,
        plan,
        [x, cot, mask, shifts, g1, b1, sb1, g2, b2, sb2]
        + [reduce_one, project_one, spatial_one, expand_one, squeeze_one, excite_one]
        + [reduce_two, spatial_two, expand_two, squeeze_two, excite_two],
        11,
        [
            b16(rows, BROAD),
            f32(4 * rows, NARROW),
            b16(4 * rows, NARROW),
            f32(rows, NARROW),
            b16(rows, NARROW),
            f32(rows, BROAD),
            f32(rows, BROAD),
            b16(rows, BROAD),
            f32(rows, NARROW),
            b16(rows, NARROW),
            f32(rows, BROAD),
            b16(rows, NARROW),
            b16(rows, BROAD),
            b16(9 * rows, NARROW),
            f32(1, 4 * NARROW + 3 * BROAD),
            f32(1, TILE),
            f32(2, BROAD + NARROW),
            f32(images, BROAD),
            f32(images, inner),
            f32(images, inner),
            f32(images, BROAD),
            f32(images, BROAD),
            f32(images, inner),
            f32(images, BROAD),
            f32(images, inner),
        ],
        [pltpu.VMEM(w.shape, BF16) for w in (reduce_one, project_one, spatial_one, expand_one)]
        + [pltpu.VMEM(w.shape, BF16) for w in (squeeze_one, excite_one, reduce_two)]
        + [pltpu.VMEM(w.shape, BF16) for w in (expand_two, squeeze_two, excite_two)]
        + [
            pltpu.VMEM((rows, BROAD), F32),
            pltpu.VMEM((rows, NARROW), F32),
            pltpu.VMEM((rows, BROAD), F32),
            pltpu.VMEM((rows, NARROW), F32),
            pltpu.VMEM((rows, NARROW), BF16),
            pltpu.VMEM((images, BROAD), F32),
            pltpu.VMEM((images, inner), F32),
            pltpu.VMEM((images, BROAD), F32),
            pltpu.VMEM((images, BROAD), F32),
            group(NARROW + BROAD + TILE),
            group(NARROW),
            group(BROAD),
            group(NARROW),
            group(NARROW),
            group(BROAD),
            group(BROAD),
            group(NARROW),
            sems((11,)),
            sems((8, n_bn - 1)),
            sems((8, n_bn - 1)),
        ],
        0,
        12 * 10**9,
    )
    (out, xa, ha, xb, hb, xc, xs, hm, xd, hd, gs, he, dzf, moved2) = first[:14]
    (scales, inverse, sums2, pool1, pre1, hid1, gate1, pool2, hid2, after2, before2) = first[14:]

    n_all = n_dp * n_bn
    thin = 8 // plan.slots
    narrow_blocks = NARROW // BLOCK
    jobs_two = []
    for k in range(BROAD // BLOCK):
        jobs_two.append(make_plain("hm", "dzd", k * BLOCK))
    for t in range(9):
        jobs_two.append(make_plain("hd", "moved", 0, None, ((8 - t) * rows, (9 - t) * rows)))
    for k in range(4):
        jobs_two.append(make_wide("he", "dzf", k * 128))
    jobs_two += [make_thin("pool", "before", thin), make_thin("after", "hidden", thin)]
    jobs_two = [(k * BLOCK, make) for k, make in enumerate(jobs_two)]
    jobs_one = []
    for k in range(image_small.shape[3] // BLOCK):
        jobs_one.append(make_plain("x", "dza", k * BLOCK))
    for t in range(9):
        i, j = t // 3, t % 3
        phase = 2 * ((i + 1) % 2) + (j + 1) % 2
        slot = 2 * (i == 0) + (j == 0)
        jobs_one.append(
            make_plain(
                "ha",
                "moved",
                0,
                (phase * rows, (phase + 1) * rows),
                (slot * rows, (slot + 1) * rows),
            )
        )
    for k in range(4):
        jobs_one.append(make_wide("hb", "dzc", k * 128))
    jobs_one += [make_thin("pool", "before", thin), make_thin("after", "hidden", thin)]
    for k in range(image_small.shape[3] // 128):
        jobs_one.append(make_wide("x", "dzs", k * 128, (0, rows)))
    jobs_one = [(k * BLOCK, make) for k, make in enumerate(jobs_one)]
    rows_one, rows_two = len(jobs_one) * BLOCK // n_all, len(jobs_two) * BLOCK // n_all
    half_one, half_two = rows_one * n_all // 2, rows_two * n_all // 2
    powers = all(s & (s - 1) == 0 and s > 1 for s in (n_dp, n_bn))
    split = powers and rows_one % 16 == 0 and rows_two % 16 == 0

    tail_two = {"hd": hd, "moved": moved2, "he": he, "dzf": dzf}
    tail_two |= {"pool": pool2, "before": before2, "after": after2, "hidden": hid2}
    if split:
        two_high = weight_grads(tail_two, jobs_two, half_two, 2 * half_two, rows_two, True)
        two_high = scatter_half(*two_high, 1, n_dp, n_bn)

    dzd, dzc, dzs, after1, before1, sums_mid = call(
        middle_kernel,
        plan,
        [mask, moved2, xd, gs, xc, xs, gate1, pre1, scales, inverse, g1, b1, g2, b2]
        + [spatial_two, reduce_two, squeeze_one, excite_one],
        4,
        [
            b16(rows, NARROW),
            b16(rows, BROAD),
            b16(rows, BROAD),
            f32(images, BROAD),
            f32(images, inner),
            f32(2, NARROW + 2 * BROAD),
        ],
        [pltpu.VMEM(w.shape, BF16) for w in (spatial_two, reduce_two, squeeze_one, excite_one)]
        + [
            pltpu.VMEM((rows, NARROW), F32),
            pltpu.VMEM((rows, BROAD), F32),
            pltpu.VMEM((images, BROAD), F32),
            pltpu.VMEM((images, BROAD), F32),
            group(NARROW),
            group(2 * BROAD),
            sems((4,)),
            sems((2, n_bn - 1)),
            sems((2, n_bn - 1)),
        ],
        1,
        4 * 10**9,
    )
    head_two = {"hm": hm, "dzd": dzd, "hd": hd, "moved": moved2}
    tail_one = {"hb": hb, "dzc": dzc, "x": x, "dzs": dzs}
    tail_one |= {"pool": pool1, "before": before1, "after": after1, "hidden": hid1}
    if split:
        two_low = weight_grads(head_two, jobs_two, 0, half_two, rows_two, True)
        two_low = scatter_half(*two_low, 0, n_dp, n_bn)
        one_high = weight_grads(tail_one, jobs_one, half_one, 2 * half_one, rows_one, True)
        one_high = scatter_half(*one_high, 1, n_dp, n_bn)

    moved1, dza, sums_one = call(
        last_kernel,
        plan,
        [mask, shifts, dzc, xb, xa, scales, inverse, g1, b1, expand_one, spatial_one],
        2,
        [b16(4 * rows, NARROW), b16(4 * rows, NARROW), f32(2, 2 * NARROW)],
        [pltpu.VMEM(w.shape, BF16) for w in (expand_one, spatial_one)]
        + [
            pltpu.VMEM((rows, NARROW), F32),
            pltpu.VMEM((rows, NARROW), BF16),
            pltpu.VMEM((4 * rows, NARROW), F32),
            group(NARROW),
            group(NARROW),
            sems((2,)),
            sems((2, n_bn - 1)),
            sems((2, n_bn - 1)),
        ],
        2,
        4 * 10**9,
    )
    head_one = {"x": x, "dza": dza, "ha": ha, "moved": moved1, "hb": hb, "dzc": dzc}
    if split:
        one_low = weight_grads(head_one, jobs_one, 0, half_one, rows_one, True)
        one_low = scatter_half(*one_low, 0, n_dp, n_bn)
        upper = lax.axis_index("dp") >= n_dp // 2
        matrices_one = jnp.where(upper, one_high, one_low).reshape(-1)
        matrices_two = jnp.where(upper, two_high, two_low).reshape(-1)
    else:
        all_two = weight_grads(tail_two | head_two, jobs_two, 0, 2 * half_two, rows_two, False)
        all_one = weight_grads(tail_one | head_one, jobs_one, 0, 2 * half_one, rows_one, False)
        matrices_one, matrices_two = (
            lax.psum_scatter(v[0].reshape(-1), ("dp", "bn"), scatter_dimension=0, tiled=True)
            for v in (all_one, all_two)
        )

    grad_x = dot_nt(dza, reduce_one).reshape(4, rows, -1)
    grad_x = jnp.concatenate([grad_x[:1] + dot_nt(dzs, project_one)[None], grad_x[1:]], axis=0)
    grad_images = plan.join_parity(grad_x)
    outputs = plan.unflatten(out)

    def bias_grad(before, after):
        return jnp.concatenate([jnp.sum(before, axis=0), jnp.sum(after, axis=0)]) / thin

    vectors = lax.psum(
        jnp.concatenate(
            [
                jnp.concatenate([sums_one, sums_mid[:, NARROW:]], axis=1).reshape(-1),
                jnp.concatenate(
                    [sums_mid[:, :NARROW], sums2[:, BROAD:], sums2[:, :BROAD]], axis=1
                ).reshape(-1),
                bias_grad(before1, after1),
                bias_grad(before2, after2),
            ]
        ),
        ("dp", "bn"),
    )
    sizes = [gains_one.size] * 2 + [gains_two.size] * 2 + [se_bias_one.size, se_bias_two.size]
    parts = []
    at = 0
    for size in sizes:
        parts.append(vectors[at : at + size])
        at += size
    shift_one, gain_one, shift_two, gain_two, bias_one, bias_two = parts
    return (
        *outputs,
        *grad_images,
        matrices_one,
        matrices_two,
        gain_one,
        shift_one,
        bias_one,
        gain_two,
        shift_two,
        bias_two,
    )


def solution(mesh):
    images = P(("dp", "bn"), None, None, None)
    return jax.shard_map(
        functools.partial(local, mesh.shape["dp"], mesh.shape["bn"]),
        mesh=mesh,
        in_specs=(images,) * 3 + (P(("dp", "bn"), None),) + (P(),) * 17 + (images,) * 3,
        out_specs=(images,) * 6 + (P(("dp", "bn")),) * 2 + (P(),) * 6,
        check_vma=False,
    )
```

```python
import functools

import jax
import jax.numpy as jnp
import numpy as np
from jax import lax
from jax.experimental import pallas as pl
from jax.experimental.pallas import tpu as pltpu
from jax.sharding import PartitionSpec as P

MESH = pl.DeviceIdType.MESH
HIGHEST = lax.Precision.HIGHEST
EPSILON = 1e-05
TILE = 256
BLOCK = 512
F32 = jnp.float32
BF16 = jnp.bfloat16
VMEM = pl.BlockSpec(memory_space=pltpu.VMEM)
ANY = pl.BlockSpec(memory_space=pl.ANY)
VMEM_BYTES = 62 * 2**20


def dot(a, b):
    return jnp.dot(a, b, preferred_element_type=F32)


def dot_nt(a, b):
    return lax.dot_general(a, b, (((1,), (1,)), ((), ())), preferred_element_type=F32)


def dot_tn(a, b):
    return lax.dot_general(a, b, (((0,), (0,)), ((), ())), preferred_element_type=F32)


def halves(a):
    high = a.astype(BF16)
    return high, (a - high.astype(F32)).astype(BF16)


def silu_slope(value):
    sigma = jax.nn.sigmoid(value)
    return sigma * (1.0 + value * (1.0 - sigma))


def total(v):
    return jnp.sum(v, axis=0, keepdims=True)


def span(j, size=TILE, start=0):
    return pl.ds(pl.multiple_of(start + j * size, 128), size)


class Plan:
    def __init__(self, images, n_bn):
        self.n = n_bn
        self.slots = images[0].shape[0]
        self.sides = [v.shape[1] // 2 for v in images]
        self.segments = []
        start = 0
        for side in self.sides:
            rows = self.slots * side * side
            padded = -(-rows // 16) * 16
            self.segments.append((start, start + padded, side, rows))
            start += padded
        self.rows = start
        shifts = np.zeros((9, start, start), np.float32)
        for begin, _, side, _ in self.segments:
            for tap in range(9):
                for r in range(side):
                    for c in range(side):
                        rr, cc = r + tap // 3 - 1, c + tap % 3 - 1
                        if 0 <= rr < side and 0 <= cc < side:
                            for k in range(self.slots):
                                here = begin + (r * side + c) * self.slots + k
                                there = begin + (rr * side + cc) * self.slots + k
                                shifts[tap, here, there] = 1.0
        self.shifts = shifts.reshape(9 * start, start)

    def mask(self, live_counts):
        pieces = []
        for k, (begin, end, _, rows) in enumerate(self.segments):
            index = jnp.arange(end - begin)
            alive = (index < rows) & (index % self.slots < live_counts[0, k])
            pieces.append(alive.astype(F32))
        return jnp.broadcast_to(jnp.concatenate(pieces)[:, None], (self.rows, TILE))

    def split_parity(self, images):
        pieces = []
        for v, (begin, end, side, rows) in zip(images, self.segments):
            v = v.transpose(1, 2, 0, 3).reshape(side, 2, side, 2, self.slots, -1)
            v = v.transpose(1, 3, 0, 2, 4, 5).reshape(4, rows, -1)
            pieces.append(jnp.pad(v, ((0, 0), (0, end - begin - rows), (0, 0))))
        return jnp.concatenate(pieces, axis=1).reshape(4 * self.rows, -1)

    def join_parity(self, flat):
        flat = flat.reshape(4, self.rows, -1)
        results = []
        for begin, _, side, rows in self.segments:
            v = flat[:, begin : begin + rows].reshape(2, 2, side, side, self.slots, -1)
            v = v.transpose(2, 0, 3, 1, 4, 5).reshape(2 * side, 2 * side, self.slots, -1)
            results.append(v.transpose(2, 0, 1, 3))
        return results

    def flatten(self, maps):
        pieces = []
        for v, (begin, end, side, rows) in zip(maps, self.segments):
            v = v.transpose(1, 2, 0, 3).reshape(rows, -1)
            pieces.append(jnp.pad(v, ((0, end - begin - rows), (0, 0))))
        return jnp.concatenate(pieces, axis=0)

    def unflatten(self, flat):
        results = []
        for begin, _, side, rows in self.segments:
            v = flat[begin : begin + rows].reshape(side, side, self.slots, -1)
            results.append(v.transpose(2, 0, 1, 3))
        return results

    def pooled(self, values):
        results = []
        for begin, end, _, _ in self.segments:
            v = values[begin:end]
            v = jnp.sum(v.reshape((end - begin) // 8, 8, v.shape[1]), axis=0)
            step = self.slots
            while step < 8:
                v = v + pltpu.roll(v, step, 0)
                step *= 2
            results.append(v)
        return results

    def spread(self, k, values, gates):
        rows, width = values.shape
        return (values.reshape(rows // 8, 8, width) * gates[None]).reshape(rows, width)


def enter(n):
    me, dp = lax.axis_index("bn"), lax.axis_index("dp")
    barrier = pltpu.get_barrier_semaphore()
    for k in range(1, n):
        pl.semaphore_signal(
            barrier, inc=1, device_id=(dp, lax.rem(me + k, n)), device_id_type=MESH
        )
    return me


def ready(n):
    pl.semaphore_wait(pltpu.get_barrier_semaphore(), n - 1)


def exchange(n, buffer, send, recv):
    me, dp = lax.axis_index("bn"), lax.axis_index("dp")
    copies = []
    for k in range(1, n):
        copies.append(
            pltpu.make_async_remote_copy(
                src_ref=buffer.at[me],
                dst_ref=buffer.at[me],
                send_sem=send.at[k - 1],
                recv_sem=recv.at[k - 1],
                device_id=(dp, lax.rem(me + k, n)),
                device_id_type=MESH,
            )
        )
    for copy in copies:
        copy.start()
    for copy in copies:
        copy.wait()


def fetch(source, target, sem):
    copy = pltpu.make_async_copy(source, target, sem)
    copy.start()
    return copy


def excite_forward(pooled, squeeze, excite, bias, pre, hidden, gate):
    inner = squeeze.shape[1]
    high, low = halves(pooled[...])
    before = dot(high, squeeze[...]) + dot(low, squeeze[...]) + bias[0:1, 0:inner]
    pre[...] = before
    after = before * jax.nn.sigmoid(before)
    hidden[...] = after
    high, low = halves(after)
    post = dot_nt(high, excite[...]) + dot_nt(low, excite[...]) + bias[0:1, inner:]
    gate[...] = jax.nn.sigmoid(post)


def excite_backward(grad_gate, gate, squeeze, excite, pre, grad_after, grad_before, grad_pooled):
    g = grad_gate[...] * gate[...] * (1.0 - gate[...])
    grad_after[...] = g
    high, low = halves(g)
    hidden = dot(high, excite[...]) + dot(low, excite[...])
    before = hidden * silu_slope(pre[...])
    grad_before[...] = before
    high, low = halves(before)
    grad_pooled[...] = dot_nt(high, squeeze[...]) + dot_nt(low, squeeze[...])


def put(buffer, me, columns, first, second):
    buffer.at[me][0:1, columns] = first
    buffer.at[me][1:2, columns] = second


def statistics(parts, mask, count):
    first = 0.0
    for v in parts:
        first = first + total(v * mask)
    mean = first / count
    second = 0.0
    for v in parts:
        d = (v - mean) * mask
        second = second + total(d * d)
    return first, second


def combine(buffer, columns, counts, level):
    n = len(counts)
    first, count = 0.0, 0.0
    for r in range(n):
        first = first + buffer[r, 0:1, columns]
        count = count + counts[r] * level
    mean = first / count
    squares = 0.0
    for r in range(n):
        own = counts[r] * level
        d = buffer[r, 0:1, columns] / own - mean
        squares = squares + buffer[r, 1:2, columns] + own * (d * d)
    return mean, lax.rsqrt(squares / count + EPSILON)


def gathered(n, buffer, columns):
    value = buffer[0, 0:2, columns]
    for r in range(1, n):
        value = value + buffer[r, 0:2, columns]
    return value[0:1], value[1:2]


def norm_back(g, xhat, mask, factor, first, second, inverse):
    return factor * (g - mask * ((first + xhat * second) * inverse))


NARROW, BROAD = 512, 2048
A, B, C, S, D, E, F = 0, 512, 1024, 3072, 5120, 5632, 6144


def forward_kernel(plan, *refs):
    (x, cot, mask, shifts, g1, b1, sb1, g2, b2, sb2) = refs[:10]
    (hr1, hp1, hs1, he1, hq1, hx1, hr2, hs2, he2, hq2, hx2) = refs[10:21]
    (out, xa, ha, xb, hb, xc, xs, hm, xd, hd, gs, he, dzf, moved) = refs[21:35]
    (scales, inverse, sums) = refs[35:38]
    (pool1, pre1, hid1, gate1, pool2, hid2, after2, before2) = refs[38:46]
    (wr1, wp1, ws, we1, wq1, wx1, wr2, we2, wq2, wx2) = refs[46:56]
    (mid, xe, xf, ge, dze, gate2, pre2, gg, gp) = refs[56:65]
    bufs = refs[65:73]
    wsem, send, recv = refs[73:]
    n, rows = plan.n, plan.rows
    me = enter(n)
    pairs = [(hr1, wr1), (hp1, wp1), (hs1, ws), (he1, we1), (hq1, wq1), (hx1, wx1)]
    pairs += [(hr2, wr2), (he2, we2), (hq2, wq2), (hx2, wx2)]
    loads = [fetch(s, t, wsem.at[k]) for k, (s, t) in enumerate(pairs)]
    m = mask[...]
    own = total(m)
    parity = [slice(p * rows, (p + 1) * rows) for p in range(4)]
    extra = pl.ds(NARROW + BROAD, TILE)
    put(bufs[0], me, extra, own, own)

    loads[0].wait()

    @pl.loop(0, NARROW // TILE)
    def _(j):
        w = wr1[:, span(j)]
        for p in parity:
            xa[p, span(j)] = dot(x[p, :], w)
        first, second = statistics([xa[p, span(j)] for p in parity], m, own * 4.0)
        put(bufs[0], me, span(j), first, second)

    loads[1].wait()

    @pl.loop(0, BROAD // TILE)
    def _(j):
        z = dot(x[parity[0], :], wp1[:, span(j)])
        xs[:, span(j)] = z
        first, second = statistics([z], m, own)
        put(bufs[0], me, span(j, start=NARROW), first, second)

    ready(n)
    exchange(n, bufs[0], send.at[0], recv.at[0])
    counts = [bufs[0][r, 0:1, extra] for r in range(n)]
    everyone = counts[0]
    for r in range(1, n):
        everyone = everyone + counts[r]
    inverse[...] = 1.0 / everyone

    @pl.loop(0, NARROW // TILE)
    def _(j):
        mean, scale = combine(bufs[0], span(j), counts, 4.0)
        scales[0:1, span(j, start=A)] = scale
        for p in parity:
            v = (xa[p, span(j)] - mean) * scale
            xa[p, span(j)] = v
            v = v * g1[0:1, span(j)] + b1[0:1, span(j)]
            ha[p, span(j)] = (v * jax.nn.sigmoid(v)).astype(BF16)

    @pl.loop(0, BROAD // TILE)
    def _(j):
        mean, scale = combine(bufs[0], span(j, start=NARROW), counts, 1.0)
        scales[0:1, span(j, start=S)] = scale
        xs[:, span(j)] = (xs[:, span(j)] - mean) * scale

    def narrow_norm(target, low, buffer, k, gain, shift, offset, where):
        @pl.loop(0, NARROW // TILE)
        def _(j):
            first, second = statistics([target[:, span(j)]], m, own)
            put(buffer, me, span(j), first, second)

        exchange(n, buffer, send.at[k], recv.at[k])

        @pl.loop(0, NARROW // TILE)
        def _(j):
            mean, scale = combine(buffer, span(j), counts, 1.0)
            scales[0:1, span(j, start=where)] = scale
            v = (target[:, span(j)] - mean) * scale
            target[:, span(j)] = v
            v = v * gain[0:1, span(j, start=offset)] + shift[0:1, span(j, start=offset)]
            low[:, span(j)] = (v * jax.nn.sigmoid(v)).astype(BF16)

    def broad_norm(source, weight, target, buffer, k, gain, shift, offset, where, pool):
        @pl.loop(0, BROAD // TILE)
        def _(j):
            z = dot(source[...], weight[:, span(j)])
            target[:, span(j)] = z
            first, second = statistics([z], m, own)
            put(buffer, me, span(j), first, second)

        exchange(n, buffer, send.at[k], recv.at[k])

        @pl.loop(0, BROAD // TILE)
        def _(j):
            mean, scale = combine(buffer, span(j), counts, 1.0)
            scales[0:1, span(j, start=where)] = scale
            v = (target[:, span(j)] - mean) * scale
            target[:, span(j)] = v
            v = v * gain[0:1, span(j, start=offset)] + shift[0:1, span(j, start=offset)]
            for k3, pooled in enumerate(plan.pooled(v * m)):
                side = plan.sides[k3]
                pool[8 * k3 : 8 * k3 + 8, span(j)] = pooled / (side * side)

    loads[2].wait()
    xb[...] = jnp.zeros_like(xb)

    @pl.loop(0, 9)
    def _(t):
        i, j = t // 3, t % 3
        phase = 2 * ((i + 1) % 2) + (j + 1) % 2
        shift = 3 * ((i + 1) // 2) + (j + 1) // 2
        moved_in = dot(
            shifts[pl.ds(pl.multiple_of(shift * rows, 16), rows), :],
            ha[pl.ds(pl.multiple_of(phase * rows, 16), rows), :],
        ).astype(BF16)
        xb[...] += dot(moved_in, ws[pl.ds(pl.multiple_of(t * NARROW, 128), NARROW), :])

    second_load = fetch(hs2, ws, wsem.at[10])
    narrow_norm(xb, hb, bufs[1], 1, g1, b1, NARROW, B)

    loads[3].wait()
    broad_norm(hb, we1, xc, bufs[2], 2, g1, b1, 2 * NARROW, C, pool1)
    loads[4].wait()
    loads[5].wait()
    excite_forward(pool1, wq1, wx1, sb1, pre1, hid1, gate1)

    @pl.loop(0, BROAD // TILE)
    def _(j):
        at, at_s = span(j, start=2 * NARROW), span(j, start=2 * NARROW + BROAD)
        for k, (a, b, _, _) in enumerate(plan.segments):
            v = xc[a:b, span(j)] * g1[0:1, at] + b1[0:1, at]
            v = plan.spread(k, v, gate1[8 * k : 8 * k + 8, span(j)])
            v = v + xs[a:b, span(j)] * g1[0:1, at_s] + b1[0:1, at_s]
            v = v * jax.nn.sigmoid(v)
            mid[a:b, span(j)] = v
            hm[a:b, span(j)] = v.astype(BF16)

    loads[6].wait()

    @pl.loop(0, NARROW // TILE)
    def _(j):
        xd[:, span(j)] = dot(hm[...], wr2[:, span(j)])

    narrow_norm(xd, hd, bufs[3], 3, g2, b2, 0, D)

    second_load.wait()
    xe[...] = jnp.zeros_like(xe)

    @pl.loop(0, 9)
    def _(t):
        moved_in = dot(
            shifts[pl.ds(pl.multiple_of(t * rows, 16), rows), :], hd[...]
        ).astype(BF16)
        xe[...] += dot(moved_in, ws[pl.ds(pl.multiple_of(t * NARROW, 128), NARROW), :])

    narrow_norm(xe, he, bufs[4], 4, g2, b2, NARROW, E)
    loads[7].wait()
    broad_norm(he, we2, xf, bufs[5], 5, g2, b2, 2 * NARROW, F, pool2)
    loads[8].wait()
    loads[9].wait()
    excite_forward(pool2, wq2, wx2, sb2, pre2, hid2, gate2)

    @pl.loop(0, BROAD // TILE)
    def _(j):
        at = span(j, start=2 * NARROW)
        for k, (a, b, _, _) in enumerate(plan.segments):
            v = xf[a:b, span(j)] * g2[0:1, at] + b2[0:1, at]
            u = plan.spread(k, v, gate2[8 * k : 8 * k + 8, span(j)]) + mid[a:b, span(j)]
            sigma = jax.nn.sigmoid(u)
            mk = mask[a:b, :]
            out[a:b, span(j)] = (u * sigma * mk).astype(BF16)
            g = cot[a:b, span(j)].astype(F32) * mk * (sigma * (1.0 + u * (1.0 - sigma)))
            gs[a:b, span(j)] = g
            mid[a:b, span(j)] = g * v
        for k, pooled in enumerate(plan.pooled(mid[:, span(j)])):
            gg[8 * k : 8 * k + 8, span(j)] = pooled

    excite_backward(gg, gate2, wq2, wx2, pre2, after2, before2, gp)

    @pl.loop(0, BROAD // TILE)
    def _(j):
        for k, (a, b, side, _) in enumerate(plan.segments):
            at = slice(8 * k, 8 * k + 8)
            g = plan.spread(k, gs[a:b, span(j)], gate2[at, span(j)])
            mid[a:b, span(j)] = g + plan.spread(
                k, mask[a:b, :], gp[at, span(j)] * (1.0 / (side * side))
            )
        g = mid[:, span(j)]
        first, second = total(g), total(g * xf[:, span(j)])
        put(bufs[6], me, span(j), first, second)
        sums[0:1, span(j)] = first
        sums[1:2, span(j)] = second

    exchange(n, bufs[6], send.at[6], recv.at[6])

    @pl.loop(0, BROAD // TILE)
    def _(j):
        first, second = gathered(n, bufs[6], span(j))
        factor = g2[0:1, span(j, start=2 * NARROW)] * scales[0:1, span(j, start=F)]
        dzf[:, span(j)] = norm_back(
            mid[:, span(j)], xf[:, span(j)], mask[...], factor, first, second, inverse[...]
        ).astype(BF16)

    @pl.loop(0, NARROW // TILE)
    def _(j):
        at = span(j, start=NARROW)
        v = xe[:, span(j)]
        g = dot_nt(dzf[...], we2[span(j), :]) * silu_slope(v * g2[0:1, at] + b2[0:1, at])
        ge[:, span(j)] = g
        first, second = total(g), total(g * v)
        put(bufs[7], me, span(j), first, second)
        sums[0:1, span(j, start=BROAD)] = first
        sums[1:2, span(j, start=BROAD)] = second

    exchange(n, bufs[7], send.at[7], recv.at[7])

    @pl.loop(0, NARROW // TILE)
    def _(j):
        first, second = gathered(n, bufs[7], span(j))
        factor = g2[0:1, span(j, start=NARROW)] * scales[0:1, span(j, start=E)]
        dze[:, span(j)] = norm_back(
            ge[:, span(j)], xe[:, span(j)], mask[...], factor, first, second, inverse[...]
        ).astype(BF16)

    @pl.loop(0, 9)
    def _(t):
        at = pl.ds(pl.multiple_of(t * rows, 16), rows)
        moved[at, :] = dot(shifts[at, :], dze[...]).astype(BF16)


def middle_kernel(plan, *refs):
    (mask, moved, xd, gs, xc, xs, gate1, pre1, scales, inverse, g1, b1, g2, b2) = refs[:14]
    (hs2, hr2, hq1, hx1) = refs[14:18]
    (dzd, dzc, dzs, after1, before1, sums) = refs[18:24]
    (ws, wr2, wq1, wx1, gd, gm, gg, gp, buf0, buf1, wsem, send, recv) = refs[24:]
    n, rows = plan.n, plan.rows
    me = enter(n)
    pairs = [(hs2, ws), (hr2, wr2), (hq1, wq1), (hx1, wx1)]
    loads = [fetch(s, t, wsem.at[k]) for k, (s, t) in enumerate(pairs)]

    loads[0].wait()
    gd[...] = jnp.zeros_like(gd)

    @pl.loop(0, 9)
    def _(t):
        gd[...] += dot_nt(
            moved[pl.ds(pl.multiple_of((8 - t) * rows, 16), rows), :],
            ws[pl.ds(pl.multiple_of(t * NARROW, 128), NARROW), :],
        )

    @pl.loop(0, NARROW // TILE)
    def _(j):
        v = xd[:, span(j)]
        g = gd[:, span(j)] * silu_slope(v * g2[0:1, span(j)] + b2[0:1, span(j)])
        gd[:, span(j)] = g
        first, second = total(g), total(g * v)
        put(buf0, me, span(j), first, second)
        sums[0:1, span(j)] = first
        sums[1:2, span(j)] = second

    ready(n)
    exchange(n, buf0, send.at[0], recv.at[0])

    @pl.loop(0, NARROW // TILE)
    def _(j):
        first, second = gathered(n, buf0, span(j))
        factor = g2[0:1, span(j)] * scales[0:1, span(j, start=D)]
        dzd[:, span(j)] = norm_back(
            gd[:, span(j)], xd[:, span(j)], mask[...], factor, first, second, inverse[...]
        ).astype(BF16)

    loads[1].wait()

    @pl.loop(0, BROAD // TILE)
    def _(j):
        at, at_s = span(j, start=2 * NARROW), span(j, start=2 * NARROW + BROAD)
        gm[:, span(j)] = gs[:, span(j)] + dot_nt(dzd[...], wr2[span(j), :])
        products = []
        for k, (a, b, _, _) in enumerate(plan.segments):
            v = xc[a:b, span(j)] * g1[0:1, at] + b1[0:1, at]
            u = plan.spread(k, v, gate1[8 * k : 8 * k + 8, span(j)])
            u = u + xs[a:b, span(j)] * g1[0:1, at_s] + b1[0:1, at_s]
            g = gm[a:b, span(j)] * silu_slope(u)
            gm[a:b, span(j)] = g
            products.append(g * v)
        for k, pooled in enumerate(plan.pooled(jnp.concatenate(products, axis=0))):
            gg[8 * k : 8 * k + 8, span(j)] = pooled
        g = gm[:, span(j)]
        first, second = total(g), total(g * xs[:, span(j)])
        put(buf1, me, span(j, start=BROAD), first, second)
        sums[0:1, span(j, start=NARROW + BROAD)] = first
        sums[1:2, span(j, start=NARROW + BROAD)] = second

    loads[2].wait()
    loads[3].wait()
    excite_backward(gg, gate1, wq1, wx1, pre1, after1, before1, gp)

    def through_gate(j):
        pieces = []
        for k, (a, b, side, _) in enumerate(plan.segments):
            at = slice(8 * k, 8 * k + 8)
            pieces.append(
                plan.spread(k, gm[a:b, span(j)], gate1[at, span(j)])
                + plan.spread(k, mask[a:b, :], gp[at, span(j)] * (1.0 / (side * side)))
            )
        return jnp.concatenate(pieces, axis=0)

    @pl.loop(0, BROAD // TILE)
    def _(j):
        g = through_gate(j)
        first, second = total(g), total(g * xc[:, span(j)])
        put(buf1, me, span(j), first, second)
        sums[0:1, span(j, start=NARROW)] = first
        sums[1:2, span(j, start=NARROW)] = second

    exchange(n, buf1, send.at[1], recv.at[1])

    @pl.loop(0, BROAD // TILE)
    def _(j):
        m, inv = mask[...], inverse[...]
        first, second = gathered(n, buf1, span(j))
        factor = g1[0:1, span(j, start=2 * NARROW)] * scales[0:1, span(j, start=C)]
        dzc[:, span(j)] = norm_back(
            through_gate(j), xc[:, span(j)], m, factor, first, second, inv
        ).astype(BF16)
        first, second = gathered(n, buf1, span(j, start=BROAD))
        factor = g1[0:1, span(j, start=2 * NARROW + BROAD)] * scales[0:1, span(j, start=S)]
        dzs[:, span(j)] = norm_back(
            gm[:, span(j)], xs[:, span(j)], m, factor, first, second, inv
        ).astype(BF16)


def last_kernel(plan, *refs):
    (mask, shifts, dzc, xb, xa, scales, inverse, g1, b1) = refs[:9]
    (he1, hs1) = refs[9:11]
    (moved, dza, sums) = refs[11:14]
    (we1, ws, gb, dzb, ga, buf0, buf1, wsem, send, recv) = refs[14:]
    n, rows = plan.n, plan.rows
    me = enter(n)
    loads = [fetch(s, t, wsem.at[k]) for k, (s, t) in enumerate([(he1, we1), (hs1, ws)])]
    loads[0].wait()

    @pl.loop(0, NARROW // TILE)
    def _(j):
        at = span(j, start=NARROW)
        v = xb[:, span(j)]
        g = dot_nt(dzc[...], we1[span(j), :]) * silu_slope(v * g1[0:1, at] + b1[0:1, at])
        gb[:, span(j)] = g
        first, second = total(g), total(g * v)
        put(buf0, me, span(j), first, second)
        sums[0:1, at] = first
        sums[1:2, at] = second

    ready(n)
    exchange(n, buf0, send.at[0], recv.at[0])

    @pl.loop(0, NARROW // TILE)
    def _(j):
        first, second = gathered(n, buf0, span(j))
        at = span(j, start=NARROW)
        factor = g1[0:1, at] * scales[0:1, span(j, start=B)]
        dzb[:, span(j)] = norm_back(
            gb[:, span(j)], xb[:, span(j)], mask[...], factor, first, second, inverse[...]
        ).astype(BF16)

    moved[0:rows, :] = dzb[...]
    for slot, tap in ((1, 5), (2, 7), (3, 8)):
        moved[slot * rows : (slot + 1) * rows, :] = dot(
            shifts[tap * rows : (tap + 1) * rows, :], dzb[...]
        ).astype(BF16)

    loads[1].wait()
    ga[...] = jnp.zeros_like(ga)

    @pl.loop(0, 9)
    def _(t):
        i, j = t // 3, t % 3
        phase = 2 * ((i + 1) % 2) + (j + 1) % 2
        slot = 2 * (1 - (i + 1) // 2) + 1 - (j + 1) // 2
        at = pl.ds(pl.multiple_of(phase * rows, 16), rows)
        ga[at, :] += dot_nt(
            moved[pl.ds(pl.multiple_of(slot * rows, 16), rows), :],
            ws[pl.ds(pl.multiple_of(t * NARROW, 128), NARROW), :],
        )

    parity = [slice(p * rows, (p + 1) * rows) for p in range(4)]

    @pl.loop(0, NARROW // TILE)
    def _(j):
        first, second = 0.0, 0.0
        for p in parity:
            v = xa[p, span(j)]
            g = ga[p, span(j)] * silu_slope(v * g1[0:1, span(j)] + b1[0:1, span(j)])
            ga[p, span(j)] = g
            first = first + total(g)
            second = second + total(g * v)
        put(buf1, me, span(j), first, second)
        sums[0:1, span(j)] = first
        sums[1:2, span(j)] = second

    exchange(n, buf1, send.at[1], recv.at[1])

    @pl.loop(0, NARROW // TILE)
    def _(j):
        first, second = gathered(n, buf1, span(j))
        factor = g1[0:1, span(j)] * scales[0:1, span(j, start=A)]
        inv = inverse[...] * 0.25
        for p in parity:
            dza[p, span(j)] = norm_back(
                ga[p, span(j)], xa[p, span(j)], mask[...], factor, first, second, inv
            ).astype(BF16)


def units_of(rows, per):
    pieces, at = [], 0
    count = -(-rows // per)
    blocks = rows // 8
    for k in range(count):
        size = (blocks * (k + 1) // count - blocks * k // count) * 8
        along = (size // 8 + (k % 2)) // 2 * 8
        pieces.append((at, along, size - along))
        at += size
    return pieces


SLOTS = 4
UNIT = 80


class Scatter:
    def __init__(self, order, rows, jobs, nz):
        self.nz = nz
        self.blocks = order
        self.rows = rows
        self.jobs = jobs
        self.units = []
        for number, (flat, b) in enumerate(order):
            for start, along, across in units_of(rows[flat], UNIT):
                self.units.append((number, flat, b, start, along, across))
        self.tall = max(rows)
        self.unit = max(u[4] + u[5] for u in self.units)
        self.part = max(max(u[4], u[5]) for u in self.units)

    def scratch(self):
        count, dma = len(self.units), pltpu.SemaphoreType.DMA
        return [
            pltpu.VMEM((5, 2, 2, self.tall, BLOCK), F32),
            pltpu.VMEM((SLOTS, 2, 2, self.unit, BLOCK), F32),
            pltpu.VMEM((SLOTS, 2, self.part, BLOCK), F32),
            pltpu.VMEM((SLOTS, 2, self.part, BLOCK), F32),
            pltpu.VMEM((SLOTS, self.part, BLOCK), F32),
            pltpu.VMEM((SLOTS, self.part, BLOCK), F32),
            pltpu.VMEM((count, self.unit, BLOCK), F32),
            pltpu.VMEM((count, self.unit, BLOCK), F32),
            pltpu.VMEM((count, self.unit, BLOCK), F32),
            pltpu.VMEM((BROAD, 128), F32),
            dma((5, SLOTS)),
            dma((5, SLOTS)),
            dma((count,)),
            dma((count,)),
            dma((count,)),
            dma((count,)),
            dma((count,)),
            pltpu.SemaphoreType.REGULAR((5,)),
        ]

    def bind(self, scratch, named, outs):
        (self.block, self.core_in, self.xa_in, self.ya_in, self.yb_in, self.xb_in) = scratch[:6]
        (self.low_in, self.high_in, self.sum, self.spare, self.sent, self.got) = scratch[6:12]
        (self.up_s, self.up_r, self.down_s, self.down_r, self.out_s, self.credit) = scratch[12:]
        self.named, self.outs = named, outs
        dp, bn = lax.axis_index("dp"), lax.axis_index("bn")
        self.core, self.x = lax.rem(bn, 2), bn // 2
        self.y, self.z = lax.rem(dp, 2), dp // 2
        self.beside = (dp, bn + 1 - 2 * self.core)
        self.along_x = (dp, bn + 2 - 4 * self.x)
        self.along_y = (dp + 1 - 2 * self.y, bn)
        self.above, self.below = (dp + 2, bn), (dp - 2, bn)
        self.copies = {}

    def greet(self):
        barrier = pltpu.get_barrier_semaphore()
        for device in (self.beside, self.along_x, self.along_y):
            pl.semaphore_signal(barrier, inc=1, device_id=device, device_id_type=MESH)

        @pl.when(self.z > 0)
        def _():
            pl.semaphore_signal(barrier, inc=1, device_id=self.below, device_id_type=MESH)

        @pl.when(self.z < self.nz - 1)
        def _():
            pl.semaphore_signal(barrier, inc=1, device_id=self.above, device_id_type=MESH)

    def met(self):
        lower = (self.z + self.nz - 1) // self.nz
        upper = (2 * self.nz - 2 - self.z) // self.nz
        pl.semaphore_wait(pltpu.get_barrier_semaphore(), 3 + lower + upper)

    def send(self, kind, u, source, target, device):
        if u >= SLOTS:
            pl.semaphore_wait(self.credit.at[kind], 1)
        slot = u % SLOTS
        copy = pltpu.make_async_remote_copy(
            src_ref=source,
            dst_ref=target,
            send_sem=self.sent.at[kind, slot],
            recv_sem=self.got.at[kind, slot],
            device_id=device,
            device_id_type=MESH,
        )
        copy.start()
        self.copies[kind, u] = copy

    def take(self, kind, u):
        self.copies.pop((kind, u)).wait()

    def release(self, kind, u, device):
        if u < len(self.units) - SLOTS:
            pl.semaphore_signal(
                self.credit.at[kind], inc=1, device_id=device, device_id_type=MESH
            )

    def tasks(self, number):
        flat, b = self.blocks[number]
        rows = self.rows[flat]
        low, high = b * 8 * rows, (b + 1) * 8 * rows
        return [j for j in self.jobs[flat] if j[0] < high and j[0] + BLOCK > low]

    def compute(self, number, job):
        flat, b = self.blocks[number]
        rows = self.rows[flat]
        start, make = job
        first = b * 8
        pieces = []
        for s in range(first, first + 8):
            a, c = max(start, s * rows), min(start + BLOCK, (s + 1) * rows)
            if a < c:
                pieces.append((s - first, a - start, c - start, a - s * rows))

        def store(begin, end, at, value):
            for s, a, c, row in pieces:
                lo, hi = max(a, begin), min(c, end)
                if lo >= hi:
                    continue
                same = 1 - lax.rem(self.core + s % 2, 2)
                index = 3 + number % 2 + (number % 3 - 3 - number % 2) * same
                target = self.block.at[index, s // 4, (s // 2) % 2]
                target[row + lo - a : row + hi - a, at] = value[lo - begin : hi - begin]

        make(self.named, store, self.spare)

    def rows_of(self, u):
        number, _, _, start, along, across = self.units[u]
        keep = self.block.at[number % 3]
        return keep, start, start + along, start + along + across, along, across

    def start_core(self, u):
        number = self.units[u][0]
        _, a, _, c, _, _ = self.rows_of(u)
        self.send(
            0,
            u,
            self.block.at[3 + number % 2, :, :, a:c],
            self.core_in.at[u % SLOTS, :, :, 0 : c - a],
            self.beside,
        )

    def finish_core(self, u):
        keep, a, b, c, along, across = self.rows_of(u)
        self.take(0, u)
        keep[:, :, a:c] += self.core_in[u % SLOTS, :, :, 0 : c - a]
        self.release(0, u, self.beside)
        self.send(
            1, u, keep.at[:, 1 - self.x, a:b], self.xa_in.at[u % SLOTS, :, 0:along], self.along_x
        )
        self.send(
            2, u, keep.at[1 - self.y, :, b:c], self.ya_in.at[u % SLOTS, :, 0:across], self.along_y
        )

    def finish_first(self, u):
        keep, a, b, c, along, across = self.rows_of(u)
        self.take(1, u)
        mine = keep.at[:, self.x]
        mine[:, a:b] += self.xa_in[u % SLOTS, :, 0:along]
        self.release(1, u, self.along_x)
        self.send(
            3,
            u,
            keep.at[1 - self.y, self.x, a:b],
            self.yb_in.at[u % SLOTS, 0:along],
            self.along_y,
        )
        self.take(2, u)
        mine = keep.at[self.y]
        mine[:, b:c] += self.ya_in[u % SLOTS, :, 0:across]
        self.release(2, u, self.along_y)
        self.send(
            4,
            u,
            keep.at[self.y, 1 - self.x, b:c],
            self.xb_in.at[u % SLOTS, 0:across],
            self.along_x,
        )

    def up(self, u):
        n = self.units[u][4] + self.units[u][5]
        return pltpu.make_async_remote_copy(
            src_ref=self.sum.at[u, 0:n],
            dst_ref=self.low_in.at[u, 0:n],
            send_sem=self.up_s.at[u],
            recv_sem=self.up_r.at[u],
            device_id=self.above,
            device_id_type=MESH,
        )

    def down(self, u):
        n = self.units[u][4] + self.units[u][5]
        return pltpu.make_async_remote_copy(
            src_ref=self.sum.at[u, 0:n],
            dst_ref=self.high_in.at[u, 0:n],
            send_sem=self.down_s.at[u],
            recv_sem=self.down_r.at[u],
            device_id=self.below,
            device_id_type=MESH,
        )

    def finish_second(self, u):
        keep, a, b, c, along, across = self.rows_of(u)
        mine = keep.at[self.y, self.x]
        self.take(3, u)
        self.sum[u, 0:along] = mine[a:b] + self.yb_in[u % SLOTS, 0:along]
        self.release(3, u, self.along_y)
        self.take(4, u)
        self.sum[u, along : along + across] = mine[b:c] + self.xb_in[u % SLOTS, 0:across]
        self.release(4, u, self.along_x)
        owner = self.units[u][2]
        if owner > 0:
            pl.when(self.z == 0)(self.up(u).start)
        if owner < self.nz - 1:
            pl.when(self.z == self.nz - 1)(self.down(u).start)

    def hop(self, u, h):
        owner = self.units[u][2]
        n = self.units[u][4] + self.units[u][5]
        if h <= owner:

            @pl.when(self.z == h)
            def _():
                self.up(u).wait_recv()
                self.sum[u, 0:n] += self.low_in[u, 0:n]
                if h < owner:
                    self.up(u).start()

        z = self.nz - 1 - h
        if z >= owner:

            @pl.when(self.z == z)
            def _():
                self.down(u).wait_recv()
                self.sum[u, 0:n] += self.high_in[u, 0:n]
                if z > owner:
                    self.down(u).start()

    def result(self, u):
        _, flat, _, start, along, across = self.units[u]
        n = along + across
        return pltpu.make_async_copy(
            self.sum.at[u, 0:n], self.outs[flat].at[start : start + n], self.out_s.at[u]
        )

    def finish(self, u):
        pl.when(self.z == self.units[u][2])(self.result(u).start)

    def settle(self):
        for u, unit in enumerate(self.units):
            owner = unit[2]

            @pl.when(self.z < owner)
            def _(u=u):
                self.up(u).wait_send()

            @pl.when(self.z > owner)
            def _(u=u):
                self.down(u).wait_send()

            @pl.when(self.z == owner)
            def _(u=u):
                self.result(u).wait()

    def steps(self):
        count = len(self.units)
        for job in self.tasks(0):
            self.compute(0, job)
        waits = 5 + 2 * self.nz
        members = {}
        for u, unit in enumerate(self.units):
            members.setdefault(unit[0], []).append(u)
        for step in range(count + waits):
            if step < count:
                self.start_core(step)
            for delay, move in ((1, self.finish_core), (3, self.finish_first), (5, self.finish_second)):
                if 0 <= step - delay < count:
                    move(step - delay)
            for h in range(1, self.nz):
                if 0 <= step - 5 - 2 * h < count:
                    self.hop(step - 5 - 2 * h, h)
            if 0 <= step - 4 - 2 * self.nz < count:
                self.finish(step - 4 - 2 * self.nz)
            if step < count:
                number = self.units[step][0]
                if number + 1 < len(self.blocks):
                    own = members[number]
                    todo = self.tasks(number + 1)
                    k = own.index(step)
                    for job in todo[len(todo) * k // len(own) : len(todo) * (k + 1) // len(own)]:
                        self.compute(number + 1, job)
            yield step
        self.settle()


class Loaded(dict):
    def __init__(self, names, sources, targets, sems):
        super().__init__()
        self.loads = {}
        for k, name in enumerate(names):
            self.loads[name] = fetch(sources[k], targets[k], sems.at[k])
            dict.__setitem__(self, name, targets[k])

    def __getitem__(self, name):
        if name in self.loads:
            self.loads.pop(name).wait()
        return dict.__getitem__(self, name)


def scatter_kernel(scatter, names, *refs):
    count = len(names)
    outs = refs[count : count + 2]
    targets = refs[count + 2 : 2 * count + 2]
    sems = refs[2 * count + 2]
    named = Loaded(names, refs[:count], targets, sems)
    scatter.bind(refs[2 * count + 3 :], named, outs)
    scatter.greet()
    steps = scatter.steps()
    scatter.met()
    for _ in steps:
        pass


def scatter_call(order, rows, jobs, nz, named, collective_id):
    scatter = Scatter(order, rows, jobs, nz)
    names = list(named)
    return pl.pallas_call(
        functools.partial(scatter_kernel, scatter, names),
        out_shape=[jax.ShapeDtypeStruct((r, BLOCK), F32) for r in rows],
        in_specs=[ANY] * len(names),
        out_specs=[ANY] * 2,
        scratch_shapes=[pltpu.VMEM(v.shape, v.dtype) for v in named.values()]
        + [pltpu.SemaphoreType.DMA((len(names),))]
        + scatter.scratch(),
        compiler_params=pltpu.CompilerParams(
            collective_id=collective_id, has_side_effects=True, vmem_limit_bytes=VMEM_BYTES
        ),
        cost_estimate=pl.CostEstimate(flops=10**10, bytes_accessed=2 * 10**8, transcendentals=0),
    )(*named.values())


def flat_kernel(names, jobs, *refs):
    named = dict(zip(names, refs[: len(names)]))
    out, stage, spare, sem = refs[len(names) :]
    copies = []
    for index, (start, make) in enumerate(jobs):
        slot = index % 2
        if index >= 2:
            copies[index - 2].wait()

        def store(begin, end, at, value):
            stage[slot, begin:end, at] = value

        make(named, store, spare)
        copies.append(fetch(stage.at[slot], out.at[start : start + BLOCK], sem.at[slot]))
    for copy in copies[-2:]:
        copy.wait()


def flat_call(named, jobs):
    return pl.pallas_call(
        functools.partial(flat_kernel, list(named), jobs),
        out_shape=jax.ShapeDtypeStruct((len(jobs) * BLOCK, BLOCK), F32),
        in_specs=[VMEM] * len(named),
        out_specs=ANY,
        scratch_shapes=[
            pltpu.VMEM((2, BLOCK, BLOCK), F32),
            pltpu.VMEM((BROAD, 128), F32),
            pltpu.SemaphoreType.DMA((2,)),
        ],
        compiler_params=pltpu.CompilerParams(vmem_limit_bytes=VMEM_BYTES),
    )(*named.values())


def make_plain(left, right, column, left_rows=None, right_rows=None):
    def make(named, store, spare):
        a, b = named[left], named[right]
        a_rows = slice(0, a.shape[0]) if left_rows is None else slice(*left_rows)
        b_rows = slice(0, b.shape[0]) if right_rows is None else slice(*right_rows)
        store(0, BLOCK, slice(0, BLOCK), dot_tn(a[a_rows, column : column + BLOCK], b[b_rows, :]))

    return make


def make_wide(left, right, column, left_rows=None):
    def make(named, store, spare):
        a, b = named[left], named[right]
        a_rows = slice(0, a.shape[0]) if left_rows is None else slice(*left_rows)
        count = BROAD // BLOCK
        lhs = a[a_rows, column : column + BLOCK // count]
        for q in range(count):
            value = dot_tn(lhs, b[:, q * BLOCK : (q + 1) * BLOCK])
            for c in range(BLOCK // 128):
                at = pl.ds(c * BLOCK + q, BLOCK // count, stride=count)
                spare[at, :] = value[:, c * 128 : (c + 1) * 128]
        for c in range(BLOCK // 128):
            store(0, BLOCK, slice(c * 128, (c + 1) * 128), spare[c * BLOCK : (c + 1) * BLOCK, :])

    return make


def make_thin(left, right, repeat):
    def make(named, store, spare):
        value = lax.dot_general(
            named[left][...],
            named[right][...],
            (((0,), (0,)), ((), ())),
            precision=HIGHEST,
            preferred_element_type=F32,
        )
        width = value.shape[1]
        count = BLOCK // width
        spare[...] = value * (1.0 / repeat)
        for q in range(count):
            at = slice(q * width, (q + 1) * width)
            store(0, BLOCK, at, spare[pl.ds(q, BLOCK, stride=count), :])

    return make


def call(kernel, plan, args, n_any, outs, scratch, collective_id, cost):
    n_vmem = len(args) - n_any
    return pl.pallas_call(
        functools.partial(kernel, plan),
        out_shape=outs,
        in_specs=[VMEM] * n_vmem + [ANY] * n_any,
        out_specs=[VMEM] * len(outs),
        scratch_shapes=scratch,
        compiler_params=pltpu.CompilerParams(
            collective_id=collective_id, has_side_effects=True, vmem_limit_bytes=VMEM_BYTES
        ),
        cost_estimate=pl.CostEstimate(flops=cost, bytes_accessed=cost // 500, transcendentals=0),
    )(*args)


def local(
    n_dp,
    n_bn,
    image_small,
    image_mid,
    image_large,
    live_counts,
    reduce_one,
    spatial_one,
    expand_one,
    squeeze_one,
    excite_one,
    project_one,
    gains_one,
    shifts_one,
    se_bias_one,
    reduce_two,
    spatial_two,
    expand_two,
    squeeze_two,
    excite_two,
    gains_two,
    shifts_two,
    se_bias_two,
    cotan_small,
    cotan_mid,
    cotan_large,
):
    plan = Plan([image_small, image_mid, image_large], n_bn)
    rows = plan.rows
    x = plan.split_parity([image_small, image_mid, image_large])
    cot = plan.flatten([cotan_small, cotan_mid, cotan_large])
    mask = plan.mask(live_counts)
    shifts = jnp.asarray(plan.shifts, BF16)
    g1, b1, sb1 = gains_one[None], shifts_one[None], se_bias_one[None]
    g2, b2, sb2 = gains_two[None], shifts_two[None], se_bias_two[None]

    def f32(*shape):
        return jax.ShapeDtypeStruct(shape, F32)

    def b16(*shape):
        return jax.ShapeDtypeStruct(shape, BF16)

    def group(width):
        return pltpu.VMEM((n_bn, 2, width), F32)

    inner = squeeze_one.shape[1]
    images = 8 * len(plan.segments)
    sems = pltpu.SemaphoreType.DMA
    first = call(
        forward_kernel,
        plan,
        [x, cot, mask, shifts, g1, b1, sb1, g2, b2, sb2]
        + [reduce_one, project_one, spatial_one, expand_one, squeeze_one, excite_one]
        + [reduce_two, spatial_two, expand_two, squeeze_two, excite_two],
        11,
        [
            b16(rows, BROAD),
            f32(4 * rows, NARROW),
            b16(4 * rows, NARROW),
            f32(rows, NARROW),
            b16(rows, NARROW),
            f32(rows, BROAD),
            f32(rows, BROAD),
            b16(rows, BROAD),
            f32(rows, NARROW),
            b16(rows, NARROW),
            f32(rows, BROAD),
            b16(rows, NARROW),
            b16(rows, BROAD),
            b16(9 * rows, NARROW),
            f32(1, 4 * NARROW + 3 * BROAD),
            f32(1, TILE),
            f32(2, BROAD + NARROW),
            f32(images, BROAD),
            f32(images, inner),
            f32(images, inner),
            f32(images, BROAD),
            f32(images, BROAD),
            f32(images, inner),
            f32(images, BROAD),
            f32(images, inner),
        ],
        [pltpu.VMEM(w.shape, BF16) for w in (reduce_one, project_one, spatial_one, expand_one)]
        + [pltpu.VMEM(w.shape, BF16) for w in (squeeze_one, excite_one, reduce_two)]
        + [pltpu.VMEM(w.shape, BF16) for w in (expand_two, squeeze_two, excite_two)]
        + [
            pltpu.VMEM((rows, BROAD), F32),
            pltpu.VMEM((rows, NARROW), F32),
            pltpu.VMEM((rows, BROAD), F32),
            pltpu.VMEM((rows, NARROW), F32),
            pltpu.VMEM((rows, NARROW), BF16),
            pltpu.VMEM((images, BROAD), F32),
            pltpu.VMEM((images, inner), F32),
            pltpu.VMEM((images, BROAD), F32),
            pltpu.VMEM((images, BROAD), F32),
            group(NARROW + BROAD + TILE),
            group(NARROW),
            group(BROAD),
            group(NARROW),
            group(NARROW),
            group(BROAD),
            group(BROAD),
            group(NARROW),
            sems((11,)),
            sems((8, n_bn - 1)),
            sems((8, n_bn - 1)),
        ],
        0,
        12 * 10**9,
    )
    (out, xa, ha, xb, hb, xc, xs, hm, xd, hd, gs, he, dzf, moved2) = first[:14]
    (scales, inverse, sums2, pool1, pre1, hid1, gate1, pool2, hid2, after2, before2) = first[14:]

    n_all = n_dp * n_bn
    thin = 8 // plan.slots
    jobs_two = []
    for k in range(BROAD // BLOCK):
        jobs_two.append(make_plain("hm", "dzd", k * BLOCK))
    for t in range(9):
        jobs_two.append(make_plain("hd", "moved", 0, None, ((8 - t) * rows, (9 - t) * rows)))
    for k in range(4):
        jobs_two.append(make_wide("he", "dzf", k * 128))
    jobs_two += [make_thin("pool2", "before2", thin), make_thin("after2", "hidden2", thin)]
    jobs_two = [(k * BLOCK, make) for k, make in enumerate(jobs_two)]
    jobs_one = []
    for k in range(image_small.shape[3] // BLOCK):
        jobs_one.append(make_plain("x", "dza", k * BLOCK))
    for t in range(9):
        i, j = t // 3, t % 3
        phase = 2 * ((i + 1) % 2) + (j + 1) % 2
        slot = 2 * (i == 0) + (j == 0)
        jobs_one.append(
            make_plain(
                "ha",
                "moved1",
                0,
                (phase * rows, (phase + 1) * rows),
                (slot * rows, (slot + 1) * rows),
            )
        )
    for k in range(4):
        jobs_one.append(make_wide("hb", "dzc", k * 128))
    jobs_one += [make_thin("pool1", "before1", thin), make_thin("after1", "hidden1", thin)]
    for k in range(image_small.shape[3] // 128):
        jobs_one.append(make_wide("x", "dzs", k * 128, (0, rows)))
    jobs_one = [(k * BLOCK, make) for k, make in enumerate(jobs_one)]
    rows_one, rows_two = len(jobs_one) * BLOCK // n_all, len(jobs_two) * BLOCK // n_all
    planned = n_bn == 4 and n_dp == 8 and rows_one % 8 == 0 and rows_two % 8 == 0

    dzd, dzc, dzs, after1, before1, sums_mid = call(
        middle_kernel,
        plan,
        [mask, moved2, xd, gs, xc, xs, gate1, pre1, scales, inverse, g1, b1, g2, b2]
        + [spatial_two, reduce_two, squeeze_one, excite_one],
        4,
        [
            b16(rows, NARROW),
            b16(rows, BROAD),
            b16(rows, BROAD),
            f32(images, BROAD),
            f32(images, inner),
            f32(2, NARROW + 2 * BROAD),
        ],
        [pltpu.VMEM(w.shape, BF16) for w in (spatial_two, reduce_two, squeeze_one, excite_one)]
        + [
            pltpu.VMEM((rows, NARROW), F32),
            pltpu.VMEM((rows, BROAD), F32),
            pltpu.VMEM((images, BROAD), F32),
            pltpu.VMEM((images, BROAD), F32),
            group(NARROW),
            group(2 * BROAD),
            sems((4,)),
            sems((2, n_bn - 1)),
            sems((2, n_bn - 1)),
        ],
        1,
        4 * 10**9,
    )
    moved1, dza, sums_one = call(
        last_kernel,
        plan,
        [mask, shifts, dzc, xb, xa, scales, inverse, g1, b1, expand_one, spatial_one],
        2,
        [b16(4 * rows, NARROW), b16(4 * rows, NARROW), f32(2, 2 * NARROW)],
        [pltpu.VMEM(w.shape, BF16) for w in (expand_one, spatial_one)]
        + [
            pltpu.VMEM((rows, NARROW), F32),
            pltpu.VMEM((rows, NARROW), BF16),
            pltpu.VMEM((4 * rows, NARROW), F32),
            group(NARROW),
            group(NARROW),
            sems((2,)),
            sems((2, n_bn - 1)),
            sems((2, n_bn - 1)),
        ],
        2,
        4 * 10**9,
    )
    named_two = {"hd": hd, "moved": moved2, "he": he, "dzf": dzf, "hm": hm, "dzd": dzd}
    named_two |= {"pool2": pool2, "before2": before2, "after2": after2, "hidden2": hid2}
    named_one = {"x": x, "dza": dza, "ha": ha, "moved1": moved1, "hb": hb, "dzc": dzc, "dzs": dzs}
    named_one |= {"pool1": pool1, "before1": before1, "after1": after1, "hidden1": hid1}
    if planned:
        order = [(1, 3), (1, 2), (1, 0), (1, 1), (0, 3), (0, 0), (0, 2), (0, 1)]
        matrices_one, matrices_two = scatter_call(
            order, (rows_one, rows_two), (jobs_one, jobs_two), n_dp // 2, named_two | named_one, 3
        )
        matrices_one, matrices_two = matrices_one.reshape(-1), matrices_two.reshape(-1)
    else:
        matrices_one, matrices_two = (
            lax.psum_scatter(v.reshape(-1), ("dp", "bn"), scatter_dimension=0, tiled=True)
            for v in (flat_call(named_one, jobs_one), flat_call(named_two, jobs_two))
        )

    grad_x = dot_nt(dza, reduce_one).reshape(4, rows, -1)
    grad_x = jnp.concatenate([grad_x[:1] + dot_nt(dzs, project_one)[None], grad_x[1:]], axis=0)
    grad_images = plan.join_parity(grad_x)
    outputs = plan.unflatten(out)

    def bias_grad(before, after):
        return jnp.concatenate([jnp.sum(before, axis=0), jnp.sum(after, axis=0)]) / thin

    vectors = lax.psum(
        jnp.concatenate(
            [
                jnp.concatenate([sums_one, sums_mid[:, NARROW:]], axis=1).reshape(-1),
                jnp.concatenate(
                    [sums_mid[:, :NARROW], sums2[:, BROAD:], sums2[:, :BROAD]], axis=1
                ).reshape(-1),
                bias_grad(before1, after1),
                bias_grad(before2, after2),
            ]
        ),
        ("dp", "bn"),
    )
    sizes = [gains_one.size] * 2 + [gains_two.size] * 2 + [se_bias_one.size, se_bias_two.size]
    parts = []
    at = 0
    for size in sizes:
        parts.append(vectors[at : at + size])
        at += size
    shift_one, gain_one, shift_two, gain_two, bias_one, bias_two = parts
    return (
        *outputs,
        *grad_images,
        matrices_one,
        matrices_two,
        gain_one,
        shift_one,
        bias_one,
        gain_two,
        shift_two,
        bias_two,
    )


def solution(mesh):
    images = P(("dp", "bn"), None, None, None)
    return jax.shard_map(
        functools.partial(local, mesh.shape["dp"], mesh.shape["bn"]),
        mesh=mesh,
        in_specs=(images,) * 3 + (P(("dp", "bn"), None),) + (P(),) * 17 + (images,) * 3,
        out_specs=(images,) * 6 + (P(("dp", "bn")),) * 2 + (P(),) * 6,
        check_vma=False,
    )
```
